32 devices in a mesh: dp: 16 (over z, x, core), blk: 2 (over y).
Axes of the slice: x: 2, y: 2, z: 4, core: 2. Of those that a mesh axis runs over, the one named last changes fastest.
Arguments:
- train_act: bfloat16 [128, 4096], P(('dp', 'blk')), may hold values from -3 to 3
- train_grad: bfloat16 [128, 8192], P(('dp', 'blk')), may hold values from -3 to 3
- query_act: bfloat16 [64, 4096], P('dp', 'blk'), may hold values from -3 to 3
- query_grad: bfloat16 [64, 8192], P('dp'), may hold values from -3 to 3
- act_basis: bfloat16 [4096, 512], P('blk'), may hold values from -0.25 to 0.25
- grad_basis: bfloat16 [512, 8192], P(None, 'dp'), may hold values from -0.25 to 0.25
- eigenvalues: float32 [4096, 8192], P('blk', 'dp'), may hold values from 0.05 to 5
- example_ids: int32 [128], replicated, may hold values from 0 to 31, never falling along the last dimension, each value on 1 to 12 neighbouring positions
- query_ids: int32 [64], replicated, may hold values from 0 to 15, never falling along the last dimension, each value on 1 to 12 neighbouring positions
Outputs:
- influence: float32 [32, 16], P('dp')
The draws below stay inside these ranges and needn't reach their ends.
Inputs may be any that keep to these rules, and one draw needn't show every extreme that they name: `example_ids`: the tokens of one training example are contiguous and ids never fall; every example has a token. `query_ids`: the tokens of one query are contiguous and ids never fall; every query has a token.
All inputs are finite; a program needn't handle non-finite values.
Results may differ from the reference program's by a relative error of at most 0.0007.
The reference program's roundings to bfloat16 on the way (of `act_rot`, `query_rot`, `grad_rot`, `query_grad_rot` and `precond`) count: a program that leaves them out, or rounds other values in their place, can miss the bound.
Values may be sent and summed in bfloat16 or wider, within the bound.
A program may use at most 64 MiB of HBM per device.

```python
import math
import jax
import jax.numpy as jnp
import numpy as np
from jax import lax

D = 4096
FF = 8192
BLOCK = 512
TOK_DEV = 4
QUERIES = 16
EX_DP = 2
TOKENS = 128
QTOKENS = 64
EXAMPLES = 32
N_BLK = 2


def shard_levels(stream_key, dims, cuts, smallest, largest):
    gain, own = 1.0, jax.random.fold_in(stream_key, 6)
    for axis_at, shards_of in cuts:
        draws = jnp.exp(jax.random.uniform(jax.random.fold_in(own, axis_at), (shards_of,), jnp.float32, smallest / len(cuts), largest / len(cuts)))
        gain = gain * jnp.repeat(draws, dims[axis_at] // shards_of).reshape([-1 if axis == axis_at else 1 for axis in range(len(dims))])
    return gain


def length_profile(count, total, most, skew):
    weights = [(1 << 20) // math.isqrt(rank ** skew) + 1 for rank in range(2, count + 1)]
    surplus, holding = total - most - (count - 1), [1] * (count - 1)
    while surplus > 0:
        free = [i for i in range(count - 1) if holding[i] < most]
        mass, budget = sum([weights[i] for i in free]), surplus
        for i in free:
            more = min(most - holding[i], max(1, budget * weights[i] // mass), surplus)
            holding[i] = holding[i] + more
            surplus = surplus - more
    return np.array([most] + holding)


def uneven(key, count, total, most, lean):
    if count == 2:
        one = jax.random.randint(key, (), max(1, total - most), min(most, total - 1) + 1)
        return jnp.stack([one, total - one])
    tallies = jnp.asarray(length_profile(count, total, most, lean), jnp.int32)
    pairs = (count - 1) // 2
    source_of, sink = tallies[1:1 + 2 * pairs:2], tallies[2:2 + 2 * pairs:2]
    slack = jnp.minimum(source_of - 1, most - sink)
    shifted = jax.random.randint(jax.random.fold_in(key, 1), (pairs,), 0, 1 << 20) % (slack + 1)
    tallies = tallies.at[1:1 + 2 * pairs:2].set(source_of - shifted).at[2:2 + 2 * pairs:2].set(sink + shifted)
    return tallies[jax.random.permutation(jax.random.fold_in(key, 2), count)]


def bell_draw(key, shape, deviation, limit, cuts=(), held_as=jnp.bfloat16):
    result = jax.random.normal(key, shape, jnp.float32) * deviation
    if len(cuts) > 0:
        result = shard_levels(key, shape, cuts, -0.22, 0.18) * result
    return jnp.clip(result, min=-limit, max=limit).astype(held_as)


def setup_inputs(seed: int = 0) -> dict:
    seeds = jax.random.split(jax.random.key(seed), 10)
    train_act = bell_draw(seeds[0], (TOKENS, D), 0.5, 3.0, ((0, 32),))
    train_grad = bell_draw(seeds[1], (TOKENS, FF), 0.5, 3.0, ((0, 32),))
    query_act = bell_draw(seeds[2], (QTOKENS, D), 0.5, 3.0, ((0, 16), (1, 2)))
    query_grad = bell_draw(seeds[3], (QTOKENS, FF), 0.5, 3.0, ((0, 16),))
    act_basis = bell_draw(seeds[4], (D, BLOCK), BLOCK ** -0.5, 0.25, ((0, 2),))
    grad_basis = bell_draw(seeds[5], (BLOCK, FF), BLOCK ** -0.5, 0.25, ((1, 16),))
    eigenvalues = jnp.clip(jnp.exp(math.log(5.0) - 4.6051702 * jax.random.uniform(seeds[6], (D, FF), jnp.float32) ** shard_levels(seeds[6], (D, FF), ((0, 2), (1, 16)), -0.2, 0.2)), 0.05, 5.0)
    example_ids = jnp.searchsorted(jnp.cumsum(uneven(seeds[7], EXAMPLES, TOKENS, 3 * TOK_DEV * N_BLK // EX_DP, 0)), jnp.arange(TOKENS), side="right").astype(jnp.int32)
    query_ids = jnp.searchsorted(jnp.cumsum(uneven(seeds[8], QUERIES, QTOKENS, 3 * QTOKENS // QUERIES, 0)), jnp.arange(QTOKENS), side="right").astype(jnp.int32)
    return {"train_act": train_act, "train_grad": train_grad, "query_act": query_act, "query_grad": query_grad, "act_basis": act_basis, "grad_basis": grad_basis, "eigenvalues": eigenvalues, "example_ids": example_ids, "query_ids": query_ids}


def round_half(values):
    return lax.optimization_barrier(values.astype(jnp.bfloat16)).astype(jnp.float32)

def reference(train_act, train_grad, query_act, query_grad, act_basis, grad_basis, eigenvalues, example_ids, query_ids):
    highest = lax.Precision.HIGHEST
    count_act = D // BLOCK
    count_grad = FF // BLOCK
    act_blocks = act_basis.astype(jnp.float32).reshape(count_act, BLOCK, BLOCK)
    grad_blocks = grad_basis.astype(jnp.float32).reshape(BLOCK, count_grad, BLOCK)

    def rotate_act(row_data):
        row_count = row_data.shape[0]
        turned = jnp.einsum('tnk,nkl->tnl', row_data.astype(jnp.float32).reshape(row_count, count_act, BLOCK), act_blocks, precision=highest)
        return round_half(turned.reshape(row_count, D))

    def rotate_grad(row_data):
        row_count = row_data.shape[0]
        turned = jnp.einsum('tnk,knl->tnl', row_data.astype(jnp.float32).reshape(row_count, count_grad, BLOCK), grad_blocks, precision=highest)
        return round_half(turned.reshape(row_count, FF))
    act_rot = rotate_act(train_act)
    query_rot = rotate_act(query_act)
    grad_rot = rotate_grad(train_grad)
    query_grad_rot = rotate_grad(query_grad)
    damping = 0.1 * jnp.sum(eigenvalues) / (D * FF)
    norm_scale = float(D * FF) ** (-0.5)
    one_query = (query_ids[:, None] == jnp.arange(QUERIES, dtype=jnp.int32)[None, :]).astype(jnp.float32)
    one_example = (example_ids[:, None] == jnp.arange(EXAMPLES, dtype=jnp.int32)[None, :]).astype(jnp.float32)

    def tile_step(summed, tile_index):
        row_start = tile_index // count_grad * BLOCK
        col_start = tile_index % count_grad * BLOCK
        act_tile = lax.dynamic_slice_in_dim(act_rot, row_start, BLOCK, 1)
        grad_tile = lax.dynamic_slice_in_dim(grad_rot, col_start, BLOCK, 1)
        query_act_tile = lax.dynamic_slice_in_dim(query_rot, row_start, BLOCK, 1)
        query_grad_tile = lax.dynamic_slice_in_dim(query_grad_rot, col_start, BLOCK, 1)
        eigen_tile = lax.dynamic_slice(eigenvalues, (row_start, col_start), (BLOCK, BLOCK))
        weighted = one_query.T[:, :, None] * query_act_tile[None, :, :]
        query_gram = jnp.einsum('qti,tj->qij', weighted, query_grad_tile, precision=highest)
        precond = round_half(query_gram / (eigen_tile[None] + damping) * norm_scale)
        mixed_rows = jnp.einsum('ti,qij->tqj', act_tile, precond, precision=highest)
        token_score = lax.optimization_barrier(jnp.sum(mixed_rows * grad_tile[:, None, :], axis=2))
        return (summed + token_score, None)
    summed, unused = lax.scan(tile_step, jnp.zeros((TOKENS, QUERIES), jnp.float32), jnp.arange(count_act * count_grad, dtype=jnp.int32))
    return jnp.dot(one_example.T, summed, precision=highest)
```

```python
import functools

import jax
import jax.numpy as jnp
from jax import lax
from jax.experimental import pallas as pl
from jax.experimental.pallas import tpu as pltpu
from jax.sharding import PartitionSpec as P

D = 4096
FF = 8192
QUERIES = 16
EX_DP = 2
MESH = pl.DeviceIdType.MESH
VMEM = pl.BlockSpec(memory_space=pltpu.VMEM)
ANY = pl.BlockSpec(memory_space=pl.ANY)


def greet_all(ndp, nblk, me):
    count = ndp * nblk
    barrier = pltpu.get_barrier_semaphore()

    @pl.loop(1, count)
    def _(k):
        to = lax.rem(me + k, count)
        pl.semaphore_signal(
            barrier, inc=1, device_id=(to // nblk, lax.rem(to, nblk)), device_id_type=MESH
        )

    pl.semaphore_wait(barrier, count - 1)


def exchange_kernel(
    ndp, nblk, ta, tg, qa, qg, eig, ta_o, tg_o, qa_o, qg_o, parts,
    eig_v, part, eig_sem, s_ta, s_tg, s_qa, s_qg, s_eig, r_sem, swap_s, swap_r,
):
    dp, blk = lax.axis_index("dp"), lax.axis_index("blk")
    half, core = dp // 2, lax.rem(dp, 2)
    me = dp * nblk + blk
    count = ndp * nblk
    nh = ndp // 2
    wa = qa.shape[1]
    wg = tg_o.shape[-1]
    load = pltpu.make_async_copy(eig, eig_v, eig_sem)
    load.start()
    greet_all(ndp, nblk, me)

    def put_ta(k):
        to = lax.rem(half * nblk + blk + k, nh * nblk)
        h, b = to // nblk, lax.rem(to, nblk)
        return pltpu.make_async_remote_copy(
            ta.at[:, pl.ds(pl.multiple_of(b * wa, 128), wa)], ta_o.at[half, core, blk],
            s_ta.at[k], r_sem.at[0], device_id=(h * 2 + core, b), device_id_type=MESH)

    def put_qa(k):
        h = lax.rem(half + k, nh)
        return pltpu.make_async_remote_copy(
            qa, qa_o.at[half, core], s_qa.at[k], r_sem.at[1],
            device_id=(h * 2 + core, blk), device_id_type=MESH)

    def put_tg(k):
        to = lax.rem(me + k, count)
        d, b = to // nblk, lax.rem(to, nblk)
        return pltpu.make_async_remote_copy(
            tg.at[:, pl.ds(pl.multiple_of(d * wg, 128), wg)], tg_o.at[me],
            s_tg.at[k], r_sem.at[2], device_id=(d, b), device_id_type=MESH)

    def put_qg(k):
        d = lax.rem(dp + k, ndp)
        return pltpu.make_async_remote_copy(
            qg.at[:, pl.ds(pl.multiple_of(d * wg, 128), wg)], qg_o.at[dp],
            s_qg.at[k], r_sem.at[3], device_id=(d, blk), device_id_type=MESH)

    def put_eig(k):
        to = lax.rem(me + k, count)
        return pltpu.make_async_remote_copy(
            part, parts.at[me], s_eig.at[k], r_sem.at[4],
            device_id=(to // nblk, lax.rem(to, nblk)), device_id_type=MESH)

    @pl.loop(1, nh)
    def _(k):
        put_qa(k).start()

    @pl.loop(1, nh * nblk)
    def _(k):
        put_ta(k).start()

    pltpu.make_async_copy(
        ta.at[:, pl.ds(pl.multiple_of(blk * wa, 128), wa)], ta_o.at[half, core, blk], r_sem.at[0]
    ).start()
    pltpu.make_async_copy(qa, qa_o.at[half, core], r_sem.at[1]).start()
    mine = pl.ds(pl.multiple_of(dp * wg, 128), wg)
    pltpu.make_async_copy(tg.at[:, mine], tg_o.at[me], r_sem.at[2]).start()
    pltpu.make_async_copy(qg.at[:, mine], qg_o.at[dp], r_sem.at[3]).start()

    load.wait()
    rows = eig_v.shape[0]
    total = jnp.zeros((8, eig_v.shape[1]), jnp.float32)

    def add(i, total):
        block = eig_v[pl.ds(pl.multiple_of(i * 256, 256), 256), :]
        return total + jnp.sum(block.reshape(32, 8, block.shape[1]), axis=0)

    total = lax.fori_loop(0, rows // 256, add, total)
    lanes = total[:, 0:128]
    for c in range(1, eig_v.shape[1] // 128):
        lanes = lanes + total[:, c * 128:(c + 1) * 128]
    part[...] = lanes

    @pl.loop(1, count)
    def _(k):
        put_eig(k).start()

    pltpu.make_async_copy(part, parts.at[me], r_sem.at[4]).start()

    @pl.loop(1, ndp)
    def _(k):
        put_qg(k).start()

    @pl.loop(1, count)
    def _(k):
        put_tg(k).start()

    def swap(buf, at):
        return pltpu.make_async_remote_copy(
            buf.at[:, core], buf.at[:, core], swap_s.at[at], swap_r.at[at],
            device_id=(half * 2 + 1 - core, blk), device_id_type=MESH)

    pltpu.make_async_copy(qa_o.at[:, core], qa_o.at[:, core], r_sem.at[1]).wait()
    swap_q = swap(qa_o, 0)
    swap_q.start()
    pltpu.make_async_copy(ta_o.at[:, core], ta_o.at[:, core], r_sem.at[0]).wait()
    swap_t = swap(ta_o, 1)
    swap_t.start()
    pltpu.make_async_copy(parts, parts, r_sem.at[4]).wait()
    pltpu.make_async_copy(qg_o, qg_o, r_sem.at[3]).wait()
    pltpu.make_async_copy(tg_o, tg_o, r_sem.at[2]).wait()

    @pl.loop(1, nh)
    def _(k):
        put_qa(k).wait_send()

    @pl.loop(1, nh * nblk)
    def _(k):
        put_ta(k).wait_send()

    @pl.loop(1, ndp)
    def _(k):
        put_qg(k).wait_send()

    @pl.loop(1, count)
    def _(k):
        put_tg(k).wait_send()
        put_eig(k).wait_send()

    swap_q.wait()
    swap_t.wait()


def exchange(ndp, nblk, ta, tg, qa, qg, eig):
    count = ndp * nblk
    nh = ndp // 2
    tok, qtok = ta.shape[0], qa.shape[0]
    wa, wg = qa.shape[1], tg.shape[1] // ndp
    bf = jnp.bfloat16
    dma = pltpu.SemaphoreType.DMA
    return pl.pallas_call(
        functools.partial(exchange_kernel, ndp, nblk),
        out_shape=(
            jax.ShapeDtypeStruct((nh, 2, nblk, tok, wa), bf),
            jax.ShapeDtypeStruct((count, tok, wg), bf),
            jax.ShapeDtypeStruct((nh, 2, qtok, wa), bf),
            jax.ShapeDtypeStruct((ndp, qtok, wg), bf),
            jax.ShapeDtypeStruct((count, 8, 128), jnp.float32),
        ),
        in_specs=[VMEM, VMEM, VMEM, VMEM, ANY],
        out_specs=(VMEM,) * 5,
        scratch_shapes=[
            pltpu.VMEM(eig.shape, jnp.float32),
            pltpu.VMEM((8, 128), jnp.float32),
            dma(()),
            dma((nh * nblk,)), dma((count,)), dma((nh,)), dma((ndp,)), dma((count,)),
            dma((5,)), dma((2,)), dma((2,)),
        ],
        compiler_params=pltpu.CompilerParams(
            collective_id=0, has_side_effects=True, vmem_limit_bytes=32 * 2**20
        ),
        name="exchange",
    )(ta, tg, qa, qg, eig)


def score_kernel(
    ta, tg, qa, qg, parts, act_basis, grad_basis, eig, qids, eids, out,
    tf, gf, qf, qgf, act, grad, query_t, qgrad, weight, score,
):
    bf, f32 = jnp.bfloat16, jnp.float32
    count, tok, wa = ta.shape
    nq, qtok, wg = qg.shape
    block = act_basis.shape[1]
    tokens = count * tok
    for s in range(count):
        tf[s * tok:(s + 1) * tok, :] = ta[s].astype(f32)
        gf[s * tok:(s + 1) * tok, :] = tg[s].astype(f32)
    for s in range(nq):
        qf[s * qtok:(s + 1) * qtok, :] = qa[s].astype(f32)
        qgf[s * qtok:(s + 1) * qtok, :] = qg[s].astype(f32)
    damping = 0.1 * jnp.sum(parts[...]) / (D * FF)
    grad[...] = jnp.dot(
        gf[...].astype(bf), grad_basis[...], preferred_element_type=f32).astype(bf).astype(f32)
    qgrad[...] = jnp.dot(
        qgf[...].astype(bf), grad_basis[...], preferred_element_type=f32).astype(bf)
    score[...] = jnp.zeros_like(score)
    norm_scale = float(D * FF) ** (-0.5)

    @pl.loop(0, wa // block)
    def _(n):
        at = pl.ds(pl.multiple_of(n * block, block), block)
        basis = act_basis[at, :]
        act[...] = jnp.dot(
            tf[:, at].astype(bf), basis, preferred_element_type=f32).astype(bf)
        turned = jnp.dot(qf[:, at].astype(bf), basis, preferred_element_type=f32)
        query_t[...] = turned.astype(bf).astype(f32).T.astype(bf)
        weight[...] = norm_scale / (eig[at, :] + damping)

        @pl.loop(0, QUERIES, unroll=2)
        def _(q):
            of_q = jnp.where(qids[...] == q, qgrad[...].astype(f32), 0.0).astype(bf)
            gram = jnp.dot(query_t[...], of_q, preferred_element_type=f32)
            precond = (gram * weight[...]).astype(bf)
            mixed = jnp.dot(act[...], precond, preferred_element_type=f32) * grad[...]
            total = mixed[:, 0:128]
            for c in range(1, wg // 128):
                total = total + mixed[:, c * 128:(c + 1) * 128]
            score[q] += total

    examples = out.shape[0] * out.shape[1]
    one = (lax.broadcasted_iota(jnp.int32, (examples, tokens), 0) == eids[...]).astype(f32)
    lane = lax.broadcasted_iota(jnp.int32, (examples, QUERIES), 1)
    result = jnp.zeros((examples, QUERIES), f32)
    for q in range(QUERIES):
        of_ex = jnp.dot(one, score[q], precision=lax.Precision.HIGHEST, preferred_element_type=f32)
        result = result + jnp.where(lane == q, jnp.sum(of_ex, axis=1, keepdims=True), 0.0)
    for d in range(out.shape[0]):
        out[d] = result[d * EX_DP:(d + 1) * EX_DP, :]


def scores(ndp, ta, tg, qa, qg, parts, act_basis, grad_basis, eig, qids, eids):
    count, tok, wa = ta.shape
    nq, qtok, wg = qg.shape
    block = act_basis.shape[1]
    tokens, qtokens = count * tok, nq * qtok
    bf, f32 = jnp.bfloat16, jnp.float32
    return pl.pallas_call(
        score_kernel,
        out_shape=jax.ShapeDtypeStruct((ndp, EX_DP, QUERIES), f32),
        in_specs=[VMEM] * 10,
        out_specs=VMEM,
        scratch_shapes=[
            pltpu.VMEM((tokens, wa), f32), pltpu.VMEM((tokens, wg), f32),
            pltpu.VMEM((qtokens, wa), f32), pltpu.VMEM((qtokens, wg), f32),
            pltpu.VMEM((tokens, block), bf), pltpu.VMEM((tokens, wg), f32),
            pltpu.VMEM((block, qtokens), bf), pltpu.VMEM((qtokens, wg), bf),
            pltpu.VMEM((block, wg), f32), pltpu.VMEM((QUERIES, tokens, 128), f32),
        ],
        compiler_params=pltpu.CompilerParams(vmem_limit_bytes=48 * 2**20),
        name="scores",
    )(ta, tg, qa, qg, parts, act_basis, grad_basis, eig, qids, eids)


def reduce_kernel(ndp, nblk, partial, out, slots, s_sem, r_sem):
    dp, blk = lax.axis_index("dp"), lax.axis_index("blk")
    me = dp * nblk + blk
    count = ndp * nblk
    greet_all(ndp, nblk, me)

    def put(k):
        to = lax.rem(me + k, count)
        d = to // nblk
        return pltpu.make_async_remote_copy(
            partial.at[d], slots.at[me], s_sem.at[k], r_sem,
            device_id=(d, lax.rem(to, nblk)), device_id_type=MESH)

    @pl.loop(1, count)
    def _(k):
        put(k).start()

    pltpu.make_async_copy(partial.at[dp], slots.at[me], r_sem).start()

    @pl.loop(1, count)
    def _(k):
        put(k).wait_send()

    pltpu.make_async_copy(slots, slots, r_sem).wait()
    out[...] = jnp.sum(slots[...], axis=0)


def reduce_scores(ndp, nblk, partial):
    count = ndp * nblk
    dma = pltpu.SemaphoreType.DMA
    return pl.pallas_call(
        functools.partial(reduce_kernel, ndp, nblk),
        out_shape=jax.ShapeDtypeStruct(partial.shape[1:], jnp.float32),
        in_specs=[VMEM],
        out_specs=VMEM,
        scratch_shapes=[
            pltpu.VMEM((count,) + partial.shape[1:], jnp.float32), dma((count,)), dma(()),
        ],
        compiler_params=pltpu.CompilerParams(collective_id=1, has_side_effects=True),
        name="reduce_scores",
    )(partial)


def shards_square(
    train_act, train_grad, query_act, query_grad, act_basis, grad_basis, eigenvalues,
    example_ids, query_ids,
):
    ndp, nblk = lax.axis_size("dp"), lax.axis_size("blk")
    ta, tg, qa, qg, parts = exchange(
        ndp, nblk, train_act, train_grad, query_act, query_grad, eigenvalues)
    ta = ta.reshape((ndp * nblk,) + ta.shape[3:])
    qa = qa.reshape((ndp,) + qa.shape[2:])
    partial = scores(
        ndp, ta, tg, qa, qg, parts, act_basis, grad_basis, eigenvalues,
        query_ids[:, None], example_ids[None, :])
    return reduce_scores(ndp, nblk, partial)


def as_sent(x):

    def short(part):
        return part.astype(jnp.bfloat16) if part.dtype == jnp.float32 else part

    return jax.tree.map(short, x)


def partner(block, axis, stride):
    count = lax.axis_size(axis)
    route = []
    for low in range(count):
        high = low | 1 << stride
        if high != low and high < count:
            route += [(low, high), (high, low)]
    return lax.ppermute(block, axis, route)


def rotate_blocks(row_data, basis):
    row_count = row_data.shape[0]
    block_size = basis.shape[1]
    count_blocks = basis.shape[0] // block_size
    turned = jnp.einsum(
        "tnk,nkl->tnl",
        row_data.reshape(row_count, count_blocks, block_size),
        basis.reshape(count_blocks, block_size, block_size),
        preferred_element_type=jnp.float32,
    )
    return turned.reshape(row_count, count_blocks * block_size).astype(jnp.bfloat16)


def rotate_columns(row_data, basis):
    row_count = row_data.shape[0]
    full_width = row_data.shape[1]
    block_size = basis.shape[0]
    col_width = basis.shape[1]
    count_blocks = full_width // block_size
    turned = jnp.einsum(
        "tmk,kml->tml",
        row_data.reshape(row_count, count_blocks, block_size),
        basis.reshape(block_size, count_blocks, col_width // count_blocks),
        preferred_element_type=jnp.float32,
    )
    return turned.reshape(row_count, col_width).astype(jnp.bfloat16)


def join_pair(mine, other, is_upper):
    return jnp.where(is_upper, jnp.concatenate([other, mine], 1), jnp.concatenate([mine, other], 1))


def shards(
    train_act,
    train_grad,
    query_act,
    query_grad,
    act_basis,
    grad_basis,
    eigenvalues,
    example_ids,
    query_ids,
):
    devices_dp = lax.axis_size("dp")
    block_size = grad_basis.shape[0]
    col_width = grad_basis.shape[1]
    owned_width = act_basis.shape[0]
    eigen_sum = lax.psum(jnp.sum(eigenvalues), ("dp", "blk"))
    damping = 0.1 * eigen_sum / (D * FF)
    owned_rows = lax.all_to_all(train_act, "blk", split_axis=1, concat_axis=0, tiled=True)
    query_all = lax.all_gather(rotate_blocks(query_act, act_basis), "dp", axis=0, tiled=True)
    train_cols, query_cols = (
        lax.all_to_all(train_grad, "dp", split_axis=1, concat_axis=0, tiled=True),
        lax.all_to_all(query_grad, "dp", split_axis=1, concat_axis=0, tiled=True),
    )
    if col_width < block_size:
        position = lax.axis_index("dp")
        for bit_index in range((block_size // col_width).bit_length() - 1):
            other_train, other_query = (
                partner(as_sent(train_cols), "dp", bit_index).astype(train_cols.dtype),
                partner(as_sent(query_cols), "dp", bit_index).astype(query_cols.dtype),
            )
            is_upper = position >> bit_index & 1 == 1
            train_cols = join_pair(train_cols, other_train, is_upper)
            query_cols = join_pair(query_cols, other_query, is_upper)
    grad_mine = rotate_columns(train_cols, grad_basis)
    query_grad_rot = rotate_columns(query_cols, grad_basis)
    grad_all = lax.all_gather(
        grad_mine.reshape(devices_dp, 1, grad_mine.shape[0] // devices_dp, col_width),
        "blk",
        axis=1,
        tiled=True,
    )
    grad_all = grad_all.reshape(
        grad_all.shape[0] * grad_all.shape[1] * grad_all.shape[2], col_width
    )
    one_query = (query_ids[:, None] == jnp.arange(QUERIES, dtype=jnp.int32)[None, :]).astype(
        jnp.bfloat16
    )
    weighted = one_query.T[:, :, None] * query_all[None, :, :]
    query_gram = jnp.einsum(
        "qti,tj->iqj", weighted, query_grad_rot, preferred_element_type=jnp.float32
    )
    norm_scale = float(D * FF) ** (-0.5)
    precond = (query_gram / (eigenvalues[:, None, :] + damping) * norm_scale).astype(jnp.bfloat16)
    precond = precond.reshape(owned_width, QUERIES * col_width)
    shard_rows = lax.all_gather(rotate_blocks(owned_rows, act_basis), "dp", axis=0, tiled=True)
    row_count = shard_rows.shape[0]
    mixed_rows = jnp.dot(shard_rows, precond, preferred_element_type=jnp.float32).reshape(
        row_count, QUERIES, col_width
    )
    token_score = jnp.sum(mixed_rows * grad_all[:, None, :].astype(jnp.float32), axis=2)
    example_count = EX_DP * devices_dp
    one_example = (
        example_ids[:, None] == jnp.arange(example_count, dtype=jnp.int32)[None, :]
    ).astype(jnp.float32)
    partial_scores = jnp.dot(one_example.T, token_score, precision=lax.Precision.HIGHEST)
    all_scores = lax.psum(partial_scores, ("dp", "blk"))
    return lax.dynamic_slice_in_dim(all_scores, lax.axis_index("dp") * EX_DP, EX_DP, 0)


def solution(mesh):
    placed = (
        P(("dp", "blk"), None),
        P(("dp", "blk"), None),
        P("dp", "blk"),
        P("dp", None),
        P("blk", None),
        P(None, "dp"),
        P("blk", "dp"),
        P(),
        P(),
    )
    ndp = mesh.shape["dp"]

    def run(*arrays):
        square = arrays[5].shape[0] * ndp == arrays[5].shape[1] and ndp % 2 == 0
        return jax.shard_map(
            shards_square if square else shards,
            mesh=mesh, in_specs=placed, out_specs=P("dp", None), check_vma=False
        )(*arrays)

    return run
```

```python
import functools

import jax
import jax.numpy as jnp
from jax import lax
from jax.experimental import pallas as pl
from jax.experimental.pallas import tpu as pltpu
from jax.sharding import PartitionSpec as P

D = 4096
FF = 8192
QUERIES = 16
EX_DP = 2
PLANE = 4
HALVES = 2
MESH = pl.DeviceIdType.MESH


def arrived(ref, sem):
    pltpu.make_async_copy(ref, ref, sem).wait()


def kernel(
    groups, nblk,
    ta, tg, qa, qg, act_basis, grad_basis, eig, qids, eids, out,
    eig_v, ab_v, gb_v, ta_o, qa_o, tg_a, qg_a, tg_o, qg_o, part, parts_a, part_b, parts_b,
    tf, gf, qf, qgf, act_t, grad_t, query_t, qmask, weight, score,
    partial, slots_a, red, slots_b,
    load_s, a_s, a_r, p_s, p_r, r_s, r_r,
):
    bf, f32 = jnp.bfloat16, jnp.float32
    dp, blk = lax.axis_index("dp"), lax.axis_index("blk")
    g, p = dp // PLANE, lax.rem(dp, PLANE)
    gb = g * nblk + blk
    column = groups * nblk
    tok, qtok = ta.shape[0], qa.shape[0]
    wa, wh, wg = qa.shape[1], ta_o.shape[-1], tg_o.shape[-1]
    block = ab_v.shape[1]
    across = lax.rem(p + 2, PLANE)
    beside = p + 1 - 2 * lax.rem(p, 2)

    loads = [pltpu.make_async_copy(src, dst, load_s.at[i]) for i, (src, dst) in enumerate(
        ((eig, eig_v), (grad_basis, gb_v), (act_basis, ab_v)))]
    for load in loads:
        load.start()

    in_column = []
    for k in range(1, column):
        to = lax.rem(gb + k, column)
        in_column.append((to // nblk, lax.rem(to, nblk)))
    in_row = [lax.rem(g + k, groups) for k in range(1, groups)]
    in_plane = [lax.rem(p + k, PLANE) for k in range(1, PLANE)]

    barrier = pltpu.get_barrier_semaphore()
    for tg_, tb in in_column:
        pl.semaphore_signal(barrier, inc=1, device_id=(tg_ * PLANE + p, tb), device_id_type=MESH)
    for tp in in_plane:
        pl.semaphore_signal(barrier, inc=1, device_id=(g * PLANE + tp, blk), device_id_type=MESH)
    pl.semaphore_wait(barrier, column - 1 + PLANE - 1)

    def remote(src, dst, send, recv, d, b):
        return pltpu.make_async_remote_copy(
            src, dst, send, recv, device_id=(d, b), device_id_type=MESH)

    def columns(at, width):
        return pl.ds(pl.multiple_of(at, 128), width)

    def send_act(h):
        for tg_ in in_row:
            remote(qa.at[:, h * wh:(h + 1) * wh], qa_o.at[h, p, g], a_s.at[h], a_r.at[h],
                   tg_ * PLANE + p, blk).start()
        pltpu.make_async_copy(
            qa.at[:, h * wh:(h + 1) * wh], qa_o.at[h, p, g], a_r.at[h]).start()
        for tg_, tb in in_column:
            remote(ta.at[:, columns(tb * wa + h * wh, wh)], ta_o.at[h, p, gb],
                   a_s.at[2 + h], a_r.at[2 + h], tg_ * PLANE + p, tb).start()
        pltpu.make_async_copy(
            ta.at[:, columns(blk * wa + h * wh, wh)], ta_o.at[h, p, gb], a_r.at[2 + h]).start()

    send_act(0)
    wide = PLANE * wg
    for tg_ in in_row:
        remote(qg.at[:, columns(tg_ * wide, wide)], qg_a.at[g], a_s.at[4], a_r.at[4],
               tg_ * PLANE + p, blk).start()
    pltpu.make_async_copy(qg.at[:, columns(g * wide, wide)], qg_a.at[g], a_r.at[4]).start()
    for tg_, tb in in_column:
        remote(tg.at[:, columns(tg_ * wide, wide)], tg_a.at[gb], a_s.at[5], a_r.at[5],
               tg_ * PLANE + p, tb).start()
    pltpu.make_async_copy(tg.at[:, columns(g * wide, wide)], tg_a.at[gb], a_r.at[5]).start()

    loads[0].wait()

    def add(i, total):
        rows = eig_v[pl.ds(pl.multiple_of(i * 128, 128), 128), :]
        return total + jnp.sum(rows.reshape(16, 8, rows.shape[1]), axis=0)

    total = lax.fori_loop(
        0, eig_v.shape[0] // 128, add, jnp.zeros((8, eig_v.shape[1]), f32))
    lanes = total[:, 0:128]
    for c in range(1, eig_v.shape[1] // 128):
        lanes = lanes + total[:, c * 128:(c + 1) * 128]
    part[...] = lanes
    for tg_, tb in in_column:
        remote(part, parts_a.at[gb], a_s.at[6], a_r.at[6], tg_ * PLANE + p, tb).start()
    pltpu.make_async_copy(part, parts_a.at[gb], a_r.at[6]).start()
    send_act(1)

    plane_sends = []

    def to_plane(src, dst, at, tp):
        copy = remote(src, dst, p_s.at[len(plane_sends)], p_r.at[at], g * PLANE + tp, blk)
        copy.start()
        plane_sends.append(copy)

    def pass_on(h):
        arrived(qa_o.at[h, p], a_r.at[h])
        to_plane(qa_o.at[h, p], qa_o.at[h, p], 12 * h, across)
        to_plane(qa_o.at[h, p], qa_o.at[h, p], 12 * h + 1, beside)
        arrived(ta_o.at[h, p], a_r.at[2 + h])
        to_plane(ta_o.at[h, p], ta_o.at[h, p], 12 * h + 2, across)
        to_plane(ta_o.at[h, p], ta_o.at[h, p], 12 * h + 3, beside)

    def pass_beside(h):
        arrived(qa_o.at[h, p], p_r.at[12 * h])
        to_plane(qa_o.at[h, across], qa_o.at[h, across], 12 * h + 4, beside)
        arrived(ta_o.at[h, p], p_r.at[12 * h + 2])
        to_plane(ta_o.at[h, across], ta_o.at[h, across], 12 * h + 5, beside)

    def take(h):
        arrived(qa_o.at[h, p], p_r.at[12 * h + 1])
        arrived(qa_o.at[h, p], p_r.at[12 * h + 4])
        arrived(ta_o.at[h, p], p_r.at[12 * h + 3])
        arrived(ta_o.at[h, p], p_r.at[12 * h + 5])

    def unpack(h):
        for q in range(PLANE):
            for e in range(groups):
                row = (e * PLANE + q) * qtok
                qf[row:row + qtok, :] = qa_o[h, q, e].astype(f32)
                for b in range(nblk):
                    row = ((e * PLANE + q) * nblk + b) * tok
                    tf[row:row + tok, :] = ta_o[h, q, e * nblk + b].astype(f32)

    pass_on(0)
    arrived(qg_a, a_r.at[4])
    for tp in in_plane:
        to_plane(qg_a.at[:, :, columns(tp * wg, wg)], qg_o.at[p], 6, tp)
    pltpu.make_async_copy(qg_a.at[:, :, columns(p * wg, wg)], qg_o.at[p], p_r.at[6]).start()
    arrived(tg_a, a_r.at[5])
    for tp in in_plane:
        to_plane(tg_a.at[:, :, columns(tp * wg, wg)], tg_o.at[p], 7, tp)
    pltpu.make_async_copy(tg_a.at[:, :, columns(p * wg, wg)], tg_o.at[p], p_r.at[7]).start()
    arrived(parts_a, a_r.at[6])
    part_b[...] = jnp.sum(parts_a[...], axis=0)
    for tp in in_plane:
        to_plane(part_b, parts_b.at[p], 8, tp)
    pltpu.make_async_copy(part_b, parts_b.at[p], p_r.at[8]).start()
    pass_beside(0)

    loads[1].wait()
    arrived(qg_o, p_r.at[6])
    arrived(tg_o, p_r.at[7])
    for q in range(PLANE):
        for e in range(groups):
            row = (e * PLANE + q) * qtok
            qgf[row:row + qtok, :] = qg_o[q, e].astype(f32)
            for b in range(nblk):
                row = ((e * PLANE + q) * nblk + b) * tok
                gf[row:row + tok, :] = tg_o[q, e * nblk + b].astype(f32)
    turned = jnp.dot(gf[...].astype(bf), gb_v[...], preferred_element_type=f32)
    grad_t[...] = turned.astype(bf).astype(f32).T.astype(bf)
    qgrad = jnp.dot(
        qgf[...].astype(bf), gb_v[...], preferred_element_type=f32).astype(bf).astype(f32)
    qtokens = qids.shape[1]
    one_query = (lax.broadcasted_iota(jnp.int32, (QUERIES, qtokens), 0) == qids[...]).astype(f32)
    same = (lax.broadcasted_iota(jnp.int32, (qtokens, qtokens), 0)
            == lax.broadcasted_iota(jnp.int32, (qtokens, qtokens), 1)).astype(f32)
    of_token = lax.dot_general(
        same.astype(bf), one_query.astype(bf), (((1,), (1,)), ((), ())),
        preferred_element_type=f32)
    for q in range(QUERIES):
        qmask[q] = (qgrad * of_token[:, q:q + 1]).astype(bf)
    score[...] = jnp.zeros_like(score)
    loads[2].wait()
    arrived(parts_b, p_r.at[8])
    damping = 0.1 * jnp.sum(parts_b[...]) / (D * FF)
    norm_scale = float(D * FF) ** (-0.5)
    chunk = 256

    def prepare(n):
        at = slice(n * block, (n + 1) * block)
        here = slice(n * block % wh, n * block % wh + block)
        basis = ab_v[at, :]
        turned = jnp.dot(tf[:, here].astype(bf), basis, preferred_element_type=f32)
        act_t[...] = turned.astype(bf).astype(f32).T
        turned = jnp.dot(qf[:, here].astype(bf), basis, preferred_element_type=f32)
        query_t[...] = turned.astype(bf).astype(f32).T.astype(bf)
        weight[...] = norm_scale / (eig_v[at, :] + damping)

    def run(first, last):
        @pl.loop(first, last, step=2)
        def _(q0):
            for q in (q0, q0 + 1):
                total = score[q]
                for c in range(0, block, chunk):
                    rows = slice(c, c + chunk)
                    gram = jnp.dot(query_t[rows, :], qmask[q], preferred_element_type=f32)
                    precond = (gram * weight[rows, :]).astype(bf)
                    mixed = jnp.dot(precond, grad_t[...], preferred_element_type=f32)
                    mixed = mixed * act_t[rows, :]
                    total = total + jnp.sum(
                        mixed.reshape(chunk // 8, 8, mixed.shape[1]), axis=0)
                score[q] = total

    take(0)
    unpack(0)
    prepare(0)
    run(0, QUERIES)
    pass_on(1)
    prepare(1)
    run(0, QUERIES // 2)
    pass_beside(1)
    run(QUERIES // 2, QUERIES)
    take(1)
    unpack(1)
    prepare(2)
    run(0, QUERIES)
    prepare(3)
    run(0, QUERIES)

    examples, tokens = partial.shape[0] * EX_DP, eids.shape[1]
    one = (lax.broadcasted_iota(jnp.int32, (examples, tokens), 0) == eids[...]).astype(f32)
    result = lax.dot_general(
        one, jnp.sum(score[...], axis=1), (((1,), (1,)), ((), ())),
        precision=lax.Precision.HIGHEST, preferred_element_type=f32)
    for d in range(partial.shape[0]):
        partial[d] = result[d * EX_DP:(d + 1) * EX_DP, :]
    for tg_, tb in in_column:
        remote(partial.at[pl.ds(tg_ * PLANE, PLANE)], slots_a.at[gb], r_s.at[0], r_r.at[0],
               tg_ * PLANE + p, tb).start()
    pltpu.make_async_copy(
        partial.at[pl.ds(g * PLANE, PLANE)], slots_a.at[gb], r_r.at[0]).start()
    for copy in plane_sends:
        copy.wait_send()
    for h in range(HALVES):
        arrived(qa_o.at[h, p, 0:groups - 1], a_s.at[h])
        arrived(ta_o.at[h, p, 0:column - 1], a_s.at[2 + h])
    arrived(qg_a.at[0:groups - 1], a_s.at[4])
    arrived(tg_a.at[0:column - 1], a_s.at[5])
    arrived(parts_a.at[0:column - 1], a_s.at[6])
    arrived(slots_a, r_r.at[0])
    red[...] = jnp.sum(slots_a[...], axis=0)
    for tp in in_plane:
        remote(red.at[tp], slots_b.at[p], r_s.at[1], r_r.at[1], g * PLANE + tp, blk).start()
    pltpu.make_async_copy(red.at[p], slots_b.at[p], r_r.at[1]).start()
    arrived(slots_a.at[0:column - 1], r_s.at[0])
    arrived(slots_b, r_r.at[1])
    arrived(slots_b.at[0:PLANE - 1], r_s.at[1])
    out[...] = jnp.sum(slots_b[...], axis=0)


def shards_square(
    ta, tg, qa, qg, act_basis, grad_basis, eig, example_ids, query_ids,
):
    ndp, nblk = lax.axis_size("dp"), lax.axis_size("blk")
    groups = ndp // PLANE
    column = groups * nblk
    tok, qtok = ta.shape[0], qa.shape[0]
    wa, wg = qa.shape[1], tg.shape[1] // ndp
    wh = wa // HALVES
    block = act_basis.shape[1]
    tokens, qtokens = ndp * nblk * tok, ndp * qtok
    bf, f32 = jnp.bfloat16, jnp.float32
    dma = pltpu.SemaphoreType.DMA
    vmem = pltpu.VMEM
    full = pl.BlockSpec(memory_space=pltpu.VMEM)
    far = pl.BlockSpec(memory_space=pl.ANY)
    return pl.pallas_call(
        functools.partial(kernel, groups, nblk),
        out_shape=jax.ShapeDtypeStruct((EX_DP, QUERIES), f32),
        in_specs=[far] * 7 + [full] * 2,
        out_specs=full,
        scratch_shapes=[
            vmem(eig.shape, f32), vmem(act_basis.shape, bf), vmem(grad_basis.shape, bf),
            vmem((HALVES, PLANE, column, tok, wh), bf),
            vmem((HALVES, PLANE, groups, qtok, wh), bf),
            vmem((column, tok, PLANE * wg), bf), vmem((groups, qtok, PLANE * wg), bf),
            vmem((PLANE, column, tok, wg), bf), vmem((PLANE, groups, qtok, wg), bf),
            vmem((8, 128), f32), vmem((column, 8, 128), f32),
            vmem((8, 128), f32), vmem((PLANE, 8, 128), f32),
            vmem((tokens, wh), f32), vmem((tokens, wg), f32),
            vmem((qtokens, wh), f32), vmem((qtokens, wg), f32),
            vmem((block, tokens), f32), vmem((wg, tokens), bf),
            vmem((block, qtokens), bf), vmem((QUERIES, qtokens, wg), bf),
            vmem((block, wg), f32), vmem((QUERIES, 8, tokens), f32),
            vmem((ndp, EX_DP, QUERIES), f32), vmem((column, PLANE, EX_DP, QUERIES), f32),
            vmem((PLANE, EX_DP, QUERIES), f32), vmem((PLANE, EX_DP, QUERIES), f32),
            dma((3,)), dma((7,)), dma((7,)), dma((32,)), dma((20,)),
            dma((2,)), dma((2,)),
        ],
        compiler_params=pltpu.CompilerParams(
            collective_id=0, has_side_effects=True, vmem_limit_bytes=56 * 2**20
        ),
        name="influence",
    )(ta, tg, qa, qg, act_basis, grad_basis, eig, query_ids[None, :], example_ids[None, :])


def as_sent(x):

    def short(part):
        return part.astype(jnp.bfloat16) if part.dtype == jnp.float32 else part

    return jax.tree.map(short, x)


def partner(block, axis, stride):
    count = lax.axis_size(axis)
    route = []
    for low in range(count):
        high = low | 1 << stride
        if high != low and high < count:
            route += [(low, high), (high, low)]
    return lax.ppermute(block, axis, route)


def rotate_blocks(row_data, basis):
    row_count = row_data.shape[0]
    block_size = basis.shape[1]
    count_blocks = basis.shape[0] // block_size
    turned = jnp.einsum(
        "tnk,nkl->tnl",
        row_data.reshape(row_count, count_blocks, block_size),
        basis.reshape(count_blocks, block_size, block_size),
        preferred_element_type=jnp.float32,
    )
    return turned.reshape(row_count, count_blocks * block_size).astype(jnp.bfloat16)


def rotate_columns(row_data, basis):
    row_count = row_data.shape[0]
    full_width = row_data.shape[1]
    block_size = basis.shape[0]
    col_width = basis.shape[1]
    count_blocks = full_width // block_size
    turned = jnp.einsum(
        "tmk,kml->tml",
        row_data.reshape(row_count, count_blocks, block_size),
        basis.reshape(block_size, count_blocks, col_width // count_blocks),
        preferred_element_type=jnp.float32,
    )
    return turned.reshape(row_count, col_width).astype(jnp.bfloat16)


def join_pair(mine, other, is_upper):
    return jnp.where(is_upper, jnp.concatenate([other, mine], 1), jnp.concatenate([mine, other], 1))


def shards(
    train_act,
    train_grad,
    query_act,
    query_grad,
    act_basis,
    grad_basis,
    eigenvalues,
    example_ids,
    query_ids,
):
    devices_dp = lax.axis_size("dp")
    block_size = grad_basis.shape[0]
    col_width = grad_basis.shape[1]
    owned_width = act_basis.shape[0]
    eigen_sum = lax.psum(jnp.sum(eigenvalues), ("dp", "blk"))
    damping = 0.1 * eigen_sum / (D * FF)
    owned_rows = lax.all_to_all(train_act, "blk", split_axis=1, concat_axis=0, tiled=True)
    query_all = lax.all_gather(rotate_blocks(query_act, act_basis), "dp", axis=0, tiled=True)
    train_cols, query_cols = (
        lax.all_to_all(train_grad, "dp", split_axis=1, concat_axis=0, tiled=True),
        lax.all_to_all(query_grad, "dp", split_axis=1, concat_axis=0, tiled=True),
    )
    if col_width < block_size:
        position = lax.axis_index("dp")
        for bit_index in range((block_size // col_width).bit_length() - 1):
            other_train, other_query = (
                partner(as_sent(train_cols), "dp", bit_index).astype(train_cols.dtype),
                partner(as_sent(query_cols), "dp", bit_index).astype(query_cols.dtype),
            )
            is_upper = position >> bit_index & 1 == 1
            train_cols = join_pair(train_cols, other_train, is_upper)
            query_cols = join_pair(query_cols, other_query, is_upper)
    grad_mine = rotate_columns(train_cols, grad_basis)
    query_grad_rot = rotate_columns(query_cols, grad_basis)
    grad_all = lax.all_gather(
        grad_mine.reshape(devices_dp, 1, grad_mine.shape[0] // devices_dp, col_width),
        "blk",
        axis=1,
        tiled=True,
    )
    grad_all = grad_all.reshape(
        grad_all.shape[0] * grad_all.shape[1] * grad_all.shape[2], col_width
    )
    one_query = (query_ids[:, None] == jnp.arange(QUERIES, dtype=jnp.int32)[None, :]).astype(
        jnp.bfloat16
    )
    weighted = one_query.T[:, :, None] * query_all[None, :, :]
    query_gram = jnp.einsum(
        "qti,tj->iqj", weighted, query_grad_rot, preferred_element_type=jnp.float32
    )
    norm_scale = float(D * FF) ** (-0.5)
    precond = (query_gram / (eigenvalues[:, None, :] + damping) * norm_scale).astype(jnp.bfloat16)
    precond = precond.reshape(owned_width, QUERIES * col_width)
    shard_rows = lax.all_gather(rotate_blocks(owned_rows, act_basis), "dp", axis=0, tiled=True)
    row_count = shard_rows.shape[0]
    mixed_rows = jnp.dot(shard_rows, precond, preferred_element_type=jnp.float32).reshape(
        row_count, QUERIES, col_width
    )
    token_score = jnp.sum(mixed_rows * grad_all[:, None, :].astype(jnp.float32), axis=2)
    example_count = EX_DP * devices_dp
    one_example = (
        example_ids[:, None] == jnp.arange(example_count, dtype=jnp.int32)[None, :]
    ).astype(jnp.float32)
    partial_scores = jnp.dot(one_example.T, token_score, precision=lax.Precision.HIGHEST)
    all_scores = lax.psum(partial_scores, ("dp", "blk"))
    return lax.dynamic_slice_in_dim(all_scores, lax.axis_index("dp") * EX_DP, EX_DP, 0)


def solution(mesh):
    placed = (
        P(("dp", "blk"), None),
        P(("dp", "blk"), None),
        P("dp", "blk"),
        P("dp", None),
        P("blk", None),
        P(None, "dp"),
        P("blk", "dp"),
        P(),
        P(),
    )
    ndp = mesh.shape["dp"]

    def run(*arrays):
        block = arrays[4].shape[1]
        square = (
            arrays[5].shape[1] == block * ndp
            and arrays[4].shape[0] == 4 * block * mesh.shape["blk"]
            and ndp % PLANE == 0
        )
        return jax.shard_map(
            shards_square if square else shards,
            mesh=mesh, in_specs=placed, out_specs=P("dp", None), check_vma=False
        )(*arrays)

    return run
```

```python
import functools

import jax
import jax.numpy as jnp
from jax import lax
from jax.experimental import pallas as pl
from jax.experimental.pallas import tpu as pltpu
from jax.sharding import PartitionSpec as P

D = 4096
FF = 8192
QUERIES = 16
EX_DP = 2
PLANE = 4
HALVES = 2
MESH = pl.DeviceIdType.MESH


def arrived(ref, sem):
    pltpu.make_async_copy(ref, ref, sem).wait()


def kernel(
    groups, nblk,
    ta, tg, qa, qg, act_basis, grad_basis, eig, qids, eids, out,
    eig_v, ab_v, gb_v, ta_o, qa_o, tg_a, qg_a, tg_o, qg_o, part, parts_a, part_b, parts_b,
    tf, gf, qf, qgf, act, grad, query_t, qmask, weight, even, odd, score,
    partial, slots_a, red, slots_b,
    load_s, a_s, a_r, p_s, p_r, r_s, r_r,
):
    bf, f32 = jnp.bfloat16, jnp.float32
    dp, blk = lax.axis_index("dp"), lax.axis_index("blk")
    g, p = dp // PLANE, lax.rem(dp, PLANE)
    gb = g * nblk + blk
    column = groups * nblk
    tok, qtok = ta.shape[0], qa.shape[0]
    wa, wh, wg = qa.shape[1], ta_o.shape[-1], tg_o.shape[-1]
    block = ab_v.shape[1]
    across = lax.rem(p + 2, PLANE)
    beside = p + 1 - 2 * lax.rem(p, 2)

    loads = [pltpu.make_async_copy(src, dst, load_s.at[i]) for i, (src, dst) in enumerate(
        ((eig, eig_v), (grad_basis, gb_v), (act_basis, ab_v)))]
    for load in loads:
        load.start()

    in_column = []
    for k in range(1, column):
        to = lax.rem(gb + k, column)
        in_column.append((to // nblk, lax.rem(to, nblk)))
    in_row = [lax.rem(g + k, groups) for k in range(1, groups)]
    in_plane = [lax.rem(p + k, PLANE) for k in range(1, PLANE)]

    barrier = pltpu.get_barrier_semaphore()
    for tg_, tb in in_column:
        pl.semaphore_signal(barrier, inc=1, device_id=(tg_ * PLANE + p, tb), device_id_type=MESH)
    for tp in in_plane:
        pl.semaphore_signal(barrier, inc=1, device_id=(g * PLANE + tp, blk), device_id_type=MESH)
    pl.semaphore_wait(barrier, column - 1 + PLANE - 1)

    def remote(src, dst, send, recv, d, b):
        return pltpu.make_async_remote_copy(
            src, dst, send, recv, device_id=(d, b), device_id_type=MESH)

    def columns(at, width):
        return pl.ds(pl.multiple_of(at, 128), width)

    def send_act(h):
        for tg_ in in_row:
            remote(qa.at[:, h * wh:(h + 1) * wh], qa_o.at[h, p, g], a_s.at[h], a_r.at[h],
                   tg_ * PLANE + p, blk).start()
        pltpu.make_async_copy(
            qa.at[:, h * wh:(h + 1) * wh], qa_o.at[h, p, g], a_r.at[h]).start()
        for tg_, tb in in_column:
            remote(ta.at[:, columns(tb * wa + h * wh, wh)], ta_o.at[h, p, gb],
                   a_s.at[2 + h], a_r.at[2 + h], tg_ * PLANE + p, tb).start()
        pltpu.make_async_copy(
            ta.at[:, columns(blk * wa + h * wh, wh)], ta_o.at[h, p, gb], a_r.at[2 + h]).start()

    send_act(0)
    wide = PLANE * wg
    for tg_ in in_row:
        remote(qg.at[:, columns(tg_ * wide, wide)], qg_a.at[g], a_s.at[4], a_r.at[4],
               tg_ * PLANE + p, blk).start()
    pltpu.make_async_copy(qg.at[:, columns(g * wide, wide)], qg_a.at[g], a_r.at[4]).start()
    for tg_, tb in in_column:
        remote(tg.at[:, columns(tg_ * wide, wide)], tg_a.at[gb], a_s.at[5], a_r.at[5],
               tg_ * PLANE + p, tb).start()
    pltpu.make_async_copy(tg.at[:, columns(g * wide, wide)], tg_a.at[gb], a_r.at[5]).start()

    loads[0].wait()

    def add(i, total):
        rows = eig_v[pl.ds(pl.multiple_of(i * 128, 128), 128), :]
        return total + jnp.sum(rows.reshape(16, 8, rows.shape[1]), axis=0)

    total = lax.fori_loop(
        0, eig_v.shape[0] // 128, add, jnp.zeros((8, eig_v.shape[1]), f32))
    lanes = total[:, 0:128]
    for c in range(1, eig_v.shape[1] // 128):
        lanes = lanes + total[:, c * 128:(c + 1) * 128]
    part[...] = lanes
    for tg_, tb in in_column:
        remote(part, parts_a.at[gb], a_s.at[6], a_r.at[6], tg_ * PLANE + p, tb).start()
    pltpu.make_async_copy(part, parts_a.at[gb], a_r.at[6]).start()
    send_act(1)

    plane_sends = []

    def to_plane(src, dst, at, tp):
        copy = remote(src, dst, p_s.at[len(plane_sends)], p_r.at[at], g * PLANE + tp, blk)
        copy.start()
        plane_sends.append(copy)

    def pass_on(h):
        arrived(qa_o.at[h, p], a_r.at[h])
        to_plane(qa_o.at[h, p], qa_o.at[h, p], 12 * h, across)
        to_plane(qa_o.at[h, p], qa_o.at[h, p], 12 * h + 1, beside)
        arrived(ta_o.at[h, p], a_r.at[2 + h])
        to_plane(ta_o.at[h, p], ta_o.at[h, p], 12 * h + 2, across)
        to_plane(ta_o.at[h, p], ta_o.at[h, p], 12 * h + 3, beside)

    def pass_beside(h):
        arrived(qa_o.at[h, p], p_r.at[12 * h])
        to_plane(qa_o.at[h, across], qa_o.at[h, across], 12 * h + 4, beside)
        arrived(ta_o.at[h, p], p_r.at[12 * h + 2])
        to_plane(ta_o.at[h, across], ta_o.at[h, across], 12 * h + 5, beside)

    def take(h):
        arrived(qa_o.at[h, p], p_r.at[12 * h + 1])
        arrived(qa_o.at[h, p], p_r.at[12 * h + 4])
        arrived(ta_o.at[h, p], p_r.at[12 * h + 3])
        arrived(ta_o.at[h, p], p_r.at[12 * h + 5])

    def unpack(h):
        for q in range(PLANE):
            for e in range(groups):
                row = (e * PLANE + q) * qtok
                qf[row:row + qtok, :] = qa_o[h, q, e].astype(f32)
                for b in range(nblk):
                    row = ((e * PLANE + q) * nblk + b) * tok
                    tf[row:row + tok, :] = ta_o[h, q, e * nblk + b].astype(f32)

    pass_on(0)
    arrived(qg_a, a_r.at[4])
    for tp in in_plane:
        to_plane(qg_a.at[:, :, columns(tp * wg, wg)], qg_o.at[p], 6, tp)
    pltpu.make_async_copy(qg_a.at[:, :, columns(p * wg, wg)], qg_o.at[p], p_r.at[6]).start()
    arrived(tg_a, a_r.at[5])
    for tp in in_plane:
        to_plane(tg_a.at[:, :, columns(tp * wg, wg)], tg_o.at[p], 7, tp)
    pltpu.make_async_copy(tg_a.at[:, :, columns(p * wg, wg)], tg_o.at[p], p_r.at[7]).start()
    arrived(parts_a, a_r.at[6])
    part_b[...] = jnp.sum(parts_a[...], axis=0)
    for tp in in_plane:
        to_plane(part_b, parts_b.at[p], 8, tp)
    pltpu.make_async_copy(part_b, parts_b.at[p], p_r.at[8]).start()
    pass_beside(0)

    loads[1].wait()
    arrived(qg_o, p_r.at[6])
    arrived(tg_o, p_r.at[7])
    for q in range(PLANE):
        for e in range(groups):
            row = (e * PLANE + q) * qtok
            qgf[row:row + qtok, :] = qg_o[q, e].astype(f32)
            for b in range(nblk):
                row = ((e * PLANE + q) * nblk + b) * tok
                gf[row:row + tok, :] = tg_o[q, e * nblk + b].astype(f32)
    turned = jnp.dot(gf[...].astype(bf), gb_v[...], preferred_element_type=f32)
    grad[...] = turned.astype(bf).astype(f32)
    qgrad = jnp.dot(
        qgf[...].astype(bf), gb_v[...], preferred_element_type=f32).astype(bf).astype(f32)
    qtokens = qids.shape[1]
    one_query = (lax.broadcasted_iota(jnp.int32, (QUERIES, qtokens), 0) == qids[...]).astype(f32)
    same = (lax.broadcasted_iota(jnp.int32, (qtokens, qtokens), 0)
            == lax.broadcasted_iota(jnp.int32, (qtokens, qtokens), 1)).astype(f32)
    of_token = lax.dot_general(
        same.astype(bf), one_query.astype(bf), (((1,), (1,)), ((), ())),
        preferred_element_type=f32)
    for q in range(QUERIES):
        qmask[q] = (qgrad * of_token[:, q:q + 1]).astype(bf)
    score[...] = jnp.zeros_like(score)
    loads[2].wait()
    arrived(parts_b, p_r.at[8])
    damping = 0.1 * jnp.sum(parts_b[...]) / (D * FF)
    norm_scale = float(D * FF) ** (-0.5)
    chunk = 256

    def prepare(n):
        at = slice(n * block, (n + 1) * block)
        here = slice(n * block % wh, n * block % wh + block)
        basis = ab_v[at, :]
        turned = jnp.dot(tf[:, here].astype(bf), basis, preferred_element_type=f32)
        act[...] = turned.astype(bf)
        turned = jnp.dot(qf[:, here].astype(bf), basis, preferred_element_type=f32)
        query_t[...] = turned.astype(bf).astype(f32).T.astype(bf)
        weight[...] = norm_scale / (eig_v[at, :] + damping)

    def precondition(q, slot, rows):
        for c in range(0, wg, chunk):
            cols = slice(c, c + chunk)
            gram = jnp.dot(query_t[rows, :], qmask[q, :, cols], preferred_element_type=f32)
            slot[rows, cols] = (gram * weight[rows, cols]).astype(bf)

    def step(q, now, later):
        mixed = None
        for c in range(0, block, chunk):
            rows = slice(c, c + chunk)
            term = jnp.dot(act[:, rows], now[rows, :], preferred_element_type=f32)
            if later is not None:
                precondition(q + 1, later, rows)
            mixed = term if mixed is None else mixed + term
        mixed = mixed * grad[...]
        total = mixed[:, 0:128]
        for c in range(128, wg, 128):
            total = total + mixed[:, c:c + 128]
        score[q] = score[q] + total

    def run(first, last, starts, ends):
        if starts:
            for c in range(0, block, chunk):
                precondition(0, even, slice(c, c + chunk))

        @pl.loop(first, last - 2 if ends else last, step=2)
        def _(q):
            step(q, even, odd)
            step(q + 1, odd, even)

        if ends:
            step(last - 2, even, odd)
            step(last - 1, odd, None)

    take(0)
    unpack(0)
    prepare(0)
    run(0, QUERIES, True, True)
    pass_on(1)
    prepare(1)
    run(0, QUERIES // 2, True, False)
    pass_beside(1)
    run(QUERIES // 2, QUERIES, False, True)
    take(1)
    unpack(1)
    prepare(2)
    run(0, QUERIES, True, True)
    prepare(3)
    run(0, QUERIES, True, True)

    examples, tokens = partial.shape[0] * EX_DP, eids.shape[1]
    one = (lax.broadcasted_iota(jnp.int32, (examples, tokens), 0) == eids[...]).astype(f32)
    result = lax.dot_general(
        one, jnp.sum(score[...], axis=2), (((1,), (1,)), ((), ())),
        precision=lax.Precision.HIGHEST, preferred_element_type=f32)
    for d in range(partial.shape[0]):
        partial[d] = result[d * EX_DP:(d + 1) * EX_DP, :]
    for tg_, tb in in_column:
        remote(partial.at[pl.ds(tg_ * PLANE, PLANE)], slots_a.at[gb], r_s.at[0], r_r.at[0],
               tg_ * PLANE + p, tb).start()
    pltpu.make_async_copy(
        partial.at[pl.ds(g * PLANE, PLANE)], slots_a.at[gb], r_r.at[0]).start()
    for copy in plane_sends:
        copy.wait_send()
    for h in range(HALVES):
        arrived(qa_o.at[h, p, 0:groups - 1], a_s.at[h])
        arrived(ta_o.at[h, p, 0:column - 1], a_s.at[2 + h])
    arrived(qg_a.at[0:groups - 1], a_s.at[4])
    arrived(tg_a.at[0:column - 1], a_s.at[5])
    arrived(parts_a.at[0:column - 1], a_s.at[6])
    arrived(slots_a, r_r.at[0])
    red[...] = jnp.sum(slots_a[...], axis=0)
    for tp in in_plane:
        remote(red.at[tp], slots_b.at[p], r_s.at[1], r_r.at[1], g * PLANE + tp, blk).start()
    pltpu.make_async_copy(red.at[p], slots_b.at[p], r_r.at[1]).start()
    arrived(slots_a.at[0:column - 1], r_s.at[0])
    arrived(slots_b, r_r.at[1])
    arrived(slots_b.at[0:PLANE - 1], r_s.at[1])
    out[...] = jnp.sum(slots_b[...], axis=0)


def shards_square(
    ta, tg, qa, qg, act_basis, grad_basis, eig, example_ids, query_ids,
):
    ndp, nblk = lax.axis_size("dp"), lax.axis_size("blk")
    groups = ndp // PLANE
    column = groups * nblk
    tok, qtok = ta.shape[0], qa.shape[0]
    wa, wg = qa.shape[1], tg.shape[1] // ndp
    wh = wa // HALVES
    block = act_basis.shape[1]
    tokens, qtokens = ndp * nblk * tok, ndp * qtok
    bf, f32 = jnp.bfloat16, jnp.float32
    dma = pltpu.SemaphoreType.DMA
    vmem = pltpu.VMEM
    full = pl.BlockSpec(memory_space=pltpu.VMEM)
    far = pl.BlockSpec(memory_space=pl.ANY)
    return pl.pallas_call(
        functools.partial(kernel, groups, nblk),
        out_shape=jax.ShapeDtypeStruct((EX_DP, QUERIES), f32),
        in_specs=[far] * 7 + [full] * 2,
        out_specs=full,
        scratch_shapes=[
            vmem(eig.shape, f32), vmem(act_basis.shape, bf), vmem(grad_basis.shape, bf),
            vmem((HALVES, PLANE, column, tok, wh), bf),
            vmem((HALVES, PLANE, groups, qtok, wh), bf),
            vmem((column, tok, PLANE * wg), bf), vmem((groups, qtok, PLANE * wg), bf),
            vmem((PLANE, column, tok, wg), bf), vmem((PLANE, groups, qtok, wg), bf),
            vmem((8, 128), f32), vmem((column, 8, 128), f32),
            vmem((8, 128), f32), vmem((PLANE, 8, 128), f32),
            vmem((tokens, wh), f32), vmem((tokens, wg), f32),
            vmem((qtokens, wh), f32), vmem((qtokens, wg), f32),
            vmem((tokens, block), bf), vmem((tokens, wg), f32),
            vmem((block, qtokens), bf), vmem((QUERIES, qtokens, wg), bf),
            vmem((block, wg), f32), vmem((block, wg), bf), vmem((block, wg), bf),
            vmem((QUERIES, tokens, 128), f32),
            vmem((ndp, EX_DP, QUERIES), f32), vmem((column, PLANE, EX_DP, QUERIES), f32),
            vmem((PLANE, EX_DP, QUERIES), f32), vmem((PLANE, EX_DP, QUERIES), f32),
            dma((3,)), dma((7,)), dma((7,)), dma((32,)), dma((20,)),
            dma((2,)), dma((2,)),
        ],
        compiler_params=pltpu.CompilerParams(
            collective_id=0, has_side_effects=True, vmem_limit_bytes=56 * 2**20
        ),
        name="influence",
    )(ta, tg, qa, qg, act_basis, grad_basis, eig, query_ids[None, :], example_ids[None, :])


def as_sent(x):

    def short(part):
        return part.astype(jnp.bfloat16) if part.dtype == jnp.float32 else part

    return jax.tree.map(short, x)


def partner(block, axis, stride):
    count = lax.axis_size(axis)
    route = []
    for low in range(count):
        high = low | 1 << stride
        if high != low and high < count:
            route += [(low, high), (high, low)]
    return lax.ppermute(block, axis, route)


def rotate_blocks(row_data, basis):
    row_count = row_data.shape[0]
    block_size = basis.shape[1]
    count_blocks = basis.shape[0] // block_size
    turned = jnp.einsum(
        "tnk,nkl->tnl",
        row_data.reshape(row_count, count_blocks, block_size),
        basis.reshape(count_blocks, block_size, block_size),
        preferred_element_type=jnp.float32,
    )
    return turned.reshape(row_count, count_blocks * block_size).astype(jnp.bfloat16)


def rotate_columns(row_data, basis):
    row_count = row_data.shape[0]
    full_width = row_data.shape[1]
    block_size = basis.shape[0]
    col_width = basis.shape[1]
    count_blocks = full_width // block_size
    turned = jnp.einsum(
        "tmk,kml->tml",
        row_data.reshape(row_count, count_blocks, block_size),
        basis.reshape(block_size, count_blocks, col_width // count_blocks),
        preferred_element_type=jnp.float32,
    )
    return turned.reshape(row_count, col_width).astype(jnp.bfloat16)


def join_pair(mine, other, is_upper):
    return jnp.where(is_upper, jnp.concatenate([other, mine], 1), jnp.concatenate([mine, other], 1))


def shards(
    train_act,
    train_grad,
    query_act,
    query_grad,
    act_basis,
    grad_basis,
    eigenvalues,
    example_ids,
    query_ids,
):
    devices_dp = lax.axis_size("dp")
    block_size = grad_basis.shape[0]
    col_width = grad_basis.shape[1]
    owned_width = act_basis.shape[0]
    eigen_sum = lax.psum(jnp.sum(eigenvalues), ("dp", "blk"))
    damping = 0.1 * eigen_sum / (D * FF)
    owned_rows = lax.all_to_all(train_act, "blk", split_axis=1, concat_axis=0, tiled=True)
    query_all = lax.all_gather(rotate_blocks(query_act, act_basis), "dp", axis=0, tiled=True)
    train_cols, query_cols = (
        lax.all_to_all(train_grad, "dp", split_axis=1, concat_axis=0, tiled=True),
        lax.all_to_all(query_grad, "dp", split_axis=1, concat_axis=0, tiled=True),
    )
    if col_width < block_size:
        position = lax.axis_index("dp")
        for bit_index in range((block_size // col_width).bit_length() - 1):
            other_train, other_query = (
                partner(as_sent(train_cols), "dp", bit_index).astype(train_cols.dtype),
                partner(as_sent(query_cols), "dp", bit_index).astype(query_cols.dtype),
            )
            is_upper = position >> bit_index & 1 == 1
            train_cols = join_pair(train_cols, other_train, is_upper)
            query_cols = join_pair(query_cols, other_query, is_upper)
    grad_mine = rotate_columns(train_cols, grad_basis)
    query_grad_rot = rotate_columns(query_cols, grad_basis)
    grad_all = lax.all_gather(
        grad_mine.reshape(devices_dp, 1, grad_mine.shape[0] // devices_dp, col_width),
        "blk",
        axis=1,
        tiled=True,
    )
    grad_all = grad_all.reshape(
        grad_all.shape[0] * grad_all.shape[1] * grad_all.shape[2], col_width
    )
    one_query = (query_ids[:, None] == jnp.arange(QUERIES, dtype=jnp.int32)[None, :]).astype(
        jnp.bfloat16
    )
    weighted = one_query.T[:, :, None] * query_all[None, :, :]
    query_gram = jnp.einsum(
        "qti,tj->iqj", weighted, query_grad_rot, preferred_element_type=jnp.float32
    )
    norm_scale = float(D * FF) ** (-0.5)
    precond = (query_gram / (eigenvalues[:, None, :] + damping) * norm_scale).astype(jnp.bfloat16)
    precond = precond.reshape(owned_width, QUERIES * col_width)
    shard_rows = lax.all_gather(rotate_blocks(owned_rows, act_basis), "dp", axis=0, tiled=True)
    row_count = shard_rows.shape[0]
    mixed_rows = jnp.dot(shard_rows, precond, preferred_element_type=jnp.float32).reshape(
        row_count, QUERIES, col_width
    )
    token_score = jnp.sum(mixed_rows * grad_all[:, None, :].astype(jnp.float32), axis=2)
    example_count = EX_DP * devices_dp
    one_example = (
        example_ids[:, None] == jnp.arange(example_count, dtype=jnp.int32)[None, :]
    ).astype(jnp.float32)
    partial_scores = jnp.dot(one_example.T, token_score, precision=lax.Precision.HIGHEST)
    all_scores = lax.psum(partial_scores, ("dp", "blk"))
    return lax.dynamic_slice_in_dim(all_scores, lax.axis_index("dp") * EX_DP, EX_DP, 0)


def solution(mesh):
    placed = (
        P(("dp", "blk"), None),
        P(("dp", "blk"), None),
        P("dp", "blk"),
        P("dp", None),
        P("blk", None),
        P(None, "dp"),
        P("blk", "dp"),
        P(),
        P(),
    )
    ndp = mesh.shape["dp"]

    def run(*arrays):
        block = arrays[4].shape[1]
        square = (
            arrays[5].shape[1] == block * ndp
            and arrays[4].shape[0] == 4 * block * mesh.shape["blk"]
            and ndp % PLANE == 0
        )
        return jax.shard_map(
            shards_square if square else shards,
            mesh=mesh, in_specs=placed, out_specs=P("dp", None), check_vma=False
        )(*arrays)

    return run
```

```python
import functools

import jax
import jax.numpy as jnp
from jax import lax
from jax.experimental import pallas as pl
from jax.experimental.pallas import tpu as pltpu
from jax.sharding import PartitionSpec as P

D = 4096
FF = 8192
QUERIES = 16
EX_DP = 2
PLANE = 4
HALVES = 2
MESH = pl.DeviceIdType.MESH


def arrived(ref, sem):
    pltpu.make_async_copy(ref, ref, sem).wait()


def kernel(
    groups, nblk,
    ta, tg, qa, qg, act_basis, grad_basis, eig, qids, eids, out,
    eig_v, ab_v, gb_v, ta_o, qa_o, tg_a, qg_a, tg_o, qg_o, part, parts_a, part_b, parts_b,
    tf, gf, qf, qgf, act, grad, query_t, qmask, weight, even, odd, score, by_query,
    partial, slots_a, red, slots_b,
    load_s, a_s, a_r, p_s, p_r, r_s, r_r,
):
    bf, f32 = jnp.bfloat16, jnp.float32
    dp, blk = lax.axis_index("dp"), lax.axis_index("blk")
    g, p = dp // PLANE, lax.rem(dp, PLANE)
    gb = g * nblk + blk
    column = groups * nblk
    tok, qtok = ta.shape[0], qa.shape[0]
    wa, wh, wg = qa.shape[1], ta_o.shape[-1], tg_o.shape[-1]
    block = ab_v.shape[1]
    across = lax.rem(p + 2, PLANE)
    beside = p + 1 - 2 * lax.rem(p, 2)

    loads = [pltpu.make_async_copy(src, dst, load_s.at[i]) for i, (src, dst) in enumerate(
        ((eig, eig_v), (grad_basis, gb_v), (act_basis, ab_v)))]
    for load in loads:
        load.start()

    in_column = []
    for k in range(1, column):
        to = lax.rem(gb + k, column)
        in_column.append((to // nblk, lax.rem(to, nblk)))
    in_row = [lax.rem(g + k, groups) for k in range(1, groups)]
    in_plane = [lax.rem(p + k, PLANE) for k in range(1, PLANE)]

    barrier = pltpu.get_barrier_semaphore()
    for tg_, tb in in_column:
        pl.semaphore_signal(barrier, inc=1, device_id=(tg_ * PLANE + p, tb), device_id_type=MESH)
    for tp in in_plane:
        pl.semaphore_signal(barrier, inc=1, device_id=(g * PLANE + tp, blk), device_id_type=MESH)
    pl.semaphore_wait(barrier, column - 1 + PLANE - 1)

    def remote(src, dst, send, recv, d, b):
        return pltpu.make_async_remote_copy(
            src, dst, send, recv, device_id=(d, b), device_id_type=MESH)

    def columns(at, width):
        return pl.ds(pl.multiple_of(at, 128), width)

    def send_act(h):
        for tg_ in in_row:
            remote(qa.at[:, h * wh:(h + 1) * wh], qa_o.at[h, p, g], a_s.at[h], a_r.at[h],
                   tg_ * PLANE + p, blk).start()
        pltpu.make_async_copy(
            qa.at[:, h * wh:(h + 1) * wh], qa_o.at[h, p, g], a_r.at[h]).start()
        for tg_, tb in in_column:
            remote(ta.at[:, columns(tb * wa + h * wh, wh)], ta_o.at[h, p, gb],
                   a_s.at[2 + h], a_r.at[2 + h], tg_ * PLANE + p, tb).start()
        pltpu.make_async_copy(
            ta.at[:, columns(blk * wa + h * wh, wh)], ta_o.at[h, p, gb], a_r.at[2 + h]).start()

    send_act(0)
    wide = PLANE * wg
    for tg_ in in_row:
        remote(qg.at[:, columns(tg_ * wide, wide)], qg_a.at[g], a_s.at[4], a_r.at[4],
               tg_ * PLANE + p, blk).start()
    pltpu.make_async_copy(qg.at[:, columns(g * wide, wide)], qg_a.at[g], a_r.at[4]).start()
    for tg_, tb in in_column:
        remote(tg.at[:, columns(tg_ * wide, wide)], tg_a.at[gb], a_s.at[5], a_r.at[5],
               tg_ * PLANE + p, tb).start()
    pltpu.make_async_copy(tg.at[:, columns(g * wide, wide)], tg_a.at[gb], a_r.at[5]).start()

    loads[0].wait()

    def add(i, total):
        rows = eig_v[pl.ds(pl.multiple_of(i * 128, 128), 128), :]
        return total + jnp.sum(rows.reshape(16, 8, rows.shape[1]), axis=0)

    total = lax.fori_loop(
        0, eig_v.shape[0] // 128, add, jnp.zeros((8, eig_v.shape[1]), f32))
    lanes = total[:, 0:128]
    for c in range(1, eig_v.shape[1] // 128):
        lanes = lanes + total[:, c * 128:(c + 1) * 128]
    part[...] = lanes
    for tg_, tb in in_column:
        remote(part, parts_a.at[gb], a_s.at[6], a_r.at[6], tg_ * PLANE + p, tb).start()
    pltpu.make_async_copy(part, parts_a.at[gb], a_r.at[6]).start()

    plane_sends = []

    def to_plane(src, dst, at, tp):
        copy = remote(src, dst, p_s.at[len(plane_sends)], p_r.at[at], g * PLANE + tp, blk)
        plane_sends.append(copy)
        return copy

    early, late = [], []
    for h in range(HALVES):
        early.append([
            to_plane(buf.at[h, p], buf.at[h, p], 12 * h + 2 * i + k, tp)
            for i, buf in enumerate((qa_o, ta_o)) for k, tp in enumerate((across, beside))])
        late.append([
            to_plane(buf.at[h, across], buf.at[h, across], 12 * h + 4 + i, beside)
            for i, buf in enumerate((qa_o, ta_o))])

    def pass_on(h):
        arrived(qa_o.at[h, p], a_r.at[h])
        early[h][0].start()
        early[h][1].start()
        arrived(ta_o.at[h, p], a_r.at[2 + h])
        early[h][2].start()
        early[h][3].start()

    def pass_beside(h):
        arrived(qa_o.at[h, p], p_r.at[12 * h])
        late[h][0].start()
        arrived(ta_o.at[h, p], p_r.at[12 * h + 2])
        late[h][1].start()

    def take(h):
        arrived(qa_o.at[h, p], p_r.at[12 * h + 1])
        arrived(qa_o.at[h, p], p_r.at[12 * h + 4])
        arrived(ta_o.at[h, p], p_r.at[12 * h + 3])
        arrived(ta_o.at[h, p], p_r.at[12 * h + 5])

    def unpack(h):
        for q in range(PLANE):
            for e in range(groups):
                row = (e * PLANE + q) * qtok
                qf[row:row + qtok, :] = qa_o[h, q, e].astype(f32)
                for b in range(nblk):
                    row = ((e * PLANE + q) * nblk + b) * tok
                    tf[row:row + tok, :] = ta_o[h, q, e * nblk + b].astype(f32)

    pass_on(0)
    arrived(qg_a, a_r.at[4])
    for tp in in_plane:
        to_plane(qg_a.at[:, :, columns(tp * wg, wg)], qg_o.at[p], 6, tp).start()
    pltpu.make_async_copy(qg_a.at[:, :, columns(p * wg, wg)], qg_o.at[p], p_r.at[6]).start()
    arrived(tg_a, a_r.at[5])
    for tp in in_plane:
        to_plane(tg_a.at[:, :, columns(tp * wg, wg)], tg_o.at[p], 7, tp).start()
    pltpu.make_async_copy(tg_a.at[:, :, columns(p * wg, wg)], tg_o.at[p], p_r.at[7]).start()
    send_act(1)
    arrived(parts_a, a_r.at[6])
    part_b[...] = jnp.sum(parts_a[...], axis=0)
    for tp in in_plane:
        to_plane(part_b, parts_b.at[p], 8, tp).start()
    pltpu.make_async_copy(part_b, parts_b.at[p], p_r.at[8]).start()
    pass_beside(0)

    loads[1].wait()
    arrived(qg_o, p_r.at[6])
    arrived(tg_o, p_r.at[7])
    for q in range(PLANE):
        for e in range(groups):
            row = (e * PLANE + q) * qtok
            qgf[row:row + qtok, :] = qg_o[q, e].astype(f32)
            for b in range(nblk):
                row = ((e * PLANE + q) * nblk + b) * tok
                gf[row:row + tok, :] = tg_o[q, e * nblk + b].astype(f32)
    turned = jnp.dot(gf[...].astype(bf), gb_v[...], preferred_element_type=f32)
    grad[...] = turned.astype(bf).astype(f32)
    qgrad = jnp.dot(
        qgf[...].astype(bf), gb_v[...], preferred_element_type=f32).astype(bf).astype(f32)
    qtokens = qids.shape[1]
    one_query = (lax.broadcasted_iota(jnp.int32, (QUERIES, qtokens), 0) == qids[...]).astype(f32)
    same = (lax.broadcasted_iota(jnp.int32, (qtokens, qtokens), 0)
            == lax.broadcasted_iota(jnp.int32, (qtokens, qtokens), 1)).astype(f32)
    of_token = lax.dot_general(
        same.astype(bf), one_query.astype(bf), (((1,), (1,)), ((), ())),
        preferred_element_type=f32)
    for q in range(QUERIES):
        qmask[q] = (qgrad * of_token[:, q:q + 1]).astype(bf)
    score[...] = jnp.zeros_like(score)
    loads[2].wait()
    arrived(parts_b, p_r.at[8])
    damping = 0.1 * jnp.sum(parts_b[...]) / (D * FF)
    norm_scale = float(D * FF) ** (-0.5)
    chunk = 256

    count_blocks = wa // block
    in_half = wh // block

    def prepare(n):
        slot = lax.rem(n, 2)
        at = pl.ds(pl.multiple_of(n * block, block), block)
        here = pl.ds(pl.multiple_of(lax.rem(n, in_half) * block, block), block)
        basis = ab_v[at, :]
        turned = jnp.dot(tf[:, here].astype(bf), basis, preferred_element_type=f32)
        act[slot] = turned.astype(bf)
        turned = jnp.dot(qf[:, here].astype(bf), basis, preferred_element_type=f32)
        query_t[slot] = turned.astype(bf).astype(f32).T.astype(bf)
        weight[slot] = norm_scale / (eig_v[at, :] + damping)

    def precondition(at, q, held, rows):
        for c in range(0, wg, chunk):
            cols = slice(c, c + chunk)
            gram = jnp.dot(query_t[at, rows, :], qmask[q, :, cols], preferred_element_type=f32)
            held[rows, cols] = (gram * weight[at, rows, cols]).astype(bf)

    def step(at, q, now, later, next_at, next_q, last):
        mixed = None
        for c in range(0, block, chunk):
            rows = slice(c, c + chunk)
            term = jnp.dot(act[at, :, rows], now[rows, :], preferred_element_type=f32)
            if later is not None:
                precondition(next_at, next_q, later, rows)
            mixed = term if mixed is None else mixed + term
        mixed = mixed * grad[...]
        total = score[q]
        for c in range(0, wg, 128):
            total = total + mixed[:, c:c + 128]
        if last:
            lane = lax.broadcasted_iota(jnp.int32, total.shape, 1)
            by_query[...] = jnp.where(
                lane == q, jnp.sum(total, axis=1, keepdims=True), by_query[...])
        else:
            score[q] = total

    def run(at, first, last, final):
        @pl.loop(first, last, step=4)
        def _(q):
            step(at, q, even, odd, at, q + 1, final)
            step(at, q + 1, odd, even, at, q + 2, final)
            step(at, q + 2, even, odd, at, q + 3, final)
            step(at, q + 3, odd, even, at, q + 4, final)

    def tail(at, final):
        q = QUERIES - 4
        step(at, q, even, odd, at, q + 1, final)
        step(at, q + 1, odd, even, at, q + 2, final)
        step(at, q + 2, even, odd, at, q + 3, final)
        step(at, q + 3, odd, None if final else even, 1 - at, 0, final)

    take(0)
    unpack(0)
    by_query[...] = jnp.zeros_like(by_query)
    prepare(0)
    for c in range(0, block, chunk):
        precondition(0, 0, even, slice(c, c + chunk))

    @pl.loop(0, count_blocks - 1)
    def _(n):
        at = lax.rem(n, 2)
        run(at, 0, QUERIES - 8, False)

        @pl.when(n == 0)
        def _():
            pass_on(1)

        @pl.when(n == 1)
        def _():
            pass_beside(1)

        run(at, QUERIES - 8, QUERIES - 4, False)

        @pl.when(n == in_half - 1)
        def _():
            take(1)
            unpack(1)

        prepare(n + 1)
        tail(at, False)

    run((count_blocks - 1) % 2, 0, QUERIES - 4, True)
    tail((count_blocks - 1) % 2, True)

    examples, tokens = partial.shape[0] * EX_DP, eids.shape[1]
    one = (lax.broadcasted_iota(jnp.int32, (examples, tokens), 0) == eids[...]).astype(f32)
    result = lax.dot_general(
        one, by_query[...], (((1,), (0,)), ((), ())),
        precision=lax.Precision.HIGHEST, preferred_element_type=f32)
    for d in range(partial.shape[0]):
        partial[d] = result[d * EX_DP:(d + 1) * EX_DP, 0:QUERIES]
    for tg_, tb in in_column:
        remote(partial.at[pl.ds(tg_ * PLANE, PLANE)], slots_a.at[gb], r_s.at[0], r_r.at[0],
               tg_ * PLANE + p, tb).start()
    pltpu.make_async_copy(
        partial.at[pl.ds(g * PLANE, PLANE)], slots_a.at[gb], r_r.at[0]).start()
    for copy in plane_sends:
        copy.wait_send()
    for h in range(HALVES):
        arrived(qa_o.at[h, p, 0:groups - 1], a_s.at[h])
        arrived(ta_o.at[h, p, 0:column - 1], a_s.at[2 + h])
    arrived(qg_a.at[0:groups - 1], a_s.at[4])
    arrived(tg_a.at[0:column - 1], a_s.at[5])
    arrived(parts_a.at[0:column - 1], a_s.at[6])
    arrived(slots_a, r_r.at[0])
    red[...] = jnp.sum(slots_a[...], axis=0)
    for tp in in_plane:
        remote(red.at[tp], slots_b.at[p], r_s.at[1], r_r.at[1], g * PLANE + tp, blk).start()
    pltpu.make_async_copy(red.at[p], slots_b.at[p], r_r.at[1]).start()
    arrived(slots_a.at[0:column - 1], r_s.at[0])
    arrived(slots_b, r_r.at[1])
    arrived(slots_b.at[0:PLANE - 1], r_s.at[1])
    out[...] = jnp.sum(slots_b[...], axis=0)


def shards_square(
    ta, tg, qa, qg, act_basis, grad_basis, eig, example_ids, query_ids,
):
    ndp, nblk = lax.axis_size("dp"), lax.axis_size("blk")
    groups = ndp // PLANE
    column = groups * nblk
    tok, qtok = ta.shape[0], qa.shape[0]
    wa, wg = qa.shape[1], tg.shape[1] // ndp
    wh = wa // HALVES
    block = act_basis.shape[1]
    tokens, qtokens = ndp * nblk * tok, ndp * qtok
    bf, f32 = jnp.bfloat16, jnp.float32
    dma = pltpu.SemaphoreType.DMA
    vmem = pltpu.VMEM
    full = pl.BlockSpec(memory_space=pltpu.VMEM)
    far = pl.BlockSpec(memory_space=pl.ANY)
    return pl.pallas_call(
        functools.partial(kernel, groups, nblk),
        out_shape=jax.ShapeDtypeStruct((EX_DP, QUERIES), f32),
        in_specs=[far] * 7 + [full] * 2,
        out_specs=full,
        scratch_shapes=[
            vmem(eig.shape, f32), vmem(act_basis.shape, bf), vmem(grad_basis.shape, bf),
            vmem((HALVES, PLANE, column, tok, wh), bf),
            vmem((HALVES, PLANE, groups, qtok, wh), bf),
            vmem((column, tok, PLANE * wg), bf), vmem((groups, qtok, PLANE * wg), bf),
            vmem((PLANE, column, tok, wg), bf), vmem((PLANE, groups, qtok, wg), bf),
            vmem((8, 128), f32), vmem((column, 8, 128), f32),
            vmem((8, 128), f32), vmem((PLANE, 8, 128), f32),
            vmem((tokens, wh), f32), vmem((tokens, wg), f32),
            vmem((qtokens, wh), f32), vmem((qtokens, wg), f32),
            vmem((2, tokens, block), bf), vmem((tokens, wg), f32),
            vmem((2, block, qtokens), bf), vmem((QUERIES, qtokens, wg), bf),
            vmem((2, block, wg), f32), vmem((block, wg), bf), vmem((block, wg), bf),
            vmem((QUERIES, tokens, 128), f32), vmem((tokens, 128), f32),
            vmem((ndp, EX_DP, QUERIES), f32), vmem((column, PLANE, EX_DP, QUERIES), f32),
            vmem((PLANE, EX_DP, QUERIES), f32), vmem((PLANE, EX_DP, QUERIES), f32),
            dma((3,)), dma((7,)), dma((7,)), dma((32,)), dma((20,)),
            dma((2,)), dma((2,)),
        ],
        compiler_params=pltpu.CompilerParams(
            collective_id=0, has_side_effects=True, vmem_limit_bytes=56 * 2**20
        ),
        name="influence",
    )(ta, tg, qa, qg, act_basis, grad_basis, eig, query_ids[None, :], example_ids[None, :])


def as_sent(x):

    def short(part):
        return part.astype(jnp.bfloat16) if part.dtype == jnp.float32 else part

    return jax.tree.map(short, x)


def partner(block, axis, stride):
    count = lax.axis_size(axis)
    route = []
    for low in range(count):
        high = low | 1 << stride
        if high != low and high < count:
            route += [(low, high), (high, low)]
    return lax.ppermute(block, axis, route)


def rotate_blocks(row_data, basis):
    row_count = row_data.shape[0]
    block_size = basis.shape[1]
    count_blocks = basis.shape[0] // block_size
    turned = jnp.einsum(
        "tnk,nkl->tnl",
        row_data.reshape(row_count, count_blocks, block_size),
        basis.reshape(count_blocks, block_size, block_size),
        preferred_element_type=jnp.float32,
    )
    return turned.reshape(row_count, count_blocks * block_size).astype(jnp.bfloat16)


def rotate_columns(row_data, basis):
    row_count = row_data.shape[0]
    full_width = row_data.shape[1]
    block_size = basis.shape[0]
    col_width = basis.shape[1]
    count_blocks = full_width // block_size
    turned = jnp.einsum(
        "tmk,kml->tml",
        row_data.reshape(row_count, count_blocks, block_size),
        basis.reshape(block_size, count_blocks, col_width // count_blocks),
        preferred_element_type=jnp.float32,
    )
    return turned.reshape(row_count, col_width).astype(jnp.bfloat16)


def join_pair(mine, other, is_upper):
    return jnp.where(is_upper, jnp.concatenate([other, mine], 1), jnp.concatenate([mine, other], 1))


def shards(
    train_act,
    train_grad,
    query_act,
    query_grad,
    act_basis,
    grad_basis,
    eigenvalues,
    example_ids,
    query_ids,
):
    devices_dp = lax.axis_size("dp")
    block_size = grad_basis.shape[0]
    col_width = grad_basis.shape[1]
    owned_width = act_basis.shape[0]
    eigen_sum = lax.psum(jnp.sum(eigenvalues), ("dp", "blk"))
    damping = 0.1 * eigen_sum / (D * FF)
    owned_rows = lax.all_to_all(train_act, "blk", split_axis=1, concat_axis=0, tiled=True)
    query_all = lax.all_gather(rotate_blocks(query_act, act_basis), "dp", axis=0, tiled=True)
    train_cols, query_cols = (
        lax.all_to_all(train_grad, "dp", split_axis=1, concat_axis=0, tiled=True),
        lax.all_to_all(query_grad, "dp", split_axis=1, concat_axis=0, tiled=True),
    )
    if col_width < block_size:
        position = lax.axis_index("dp")
        for bit_index in range((block_size // col_width).bit_length() - 1):
            other_train, other_query = (
                partner(as_sent(train_cols), "dp", bit_index).astype(train_cols.dtype),
                partner(as_sent(query_cols), "dp", bit_index).astype(query_cols.dtype),
            )
            is_upper = position >> bit_index & 1 == 1
            train_cols = join_pair(train_cols, other_train, is_upper)
            query_cols = join_pair(query_cols, other_query, is_upper)
    grad_mine = rotate_columns(train_cols, grad_basis)
    query_grad_rot = rotate_columns(query_cols, grad_basis)
    grad_all = lax.all_gather(
        grad_mine.reshape(devices_dp, 1, grad_mine.shape[0] // devices_dp, col_width),
        "blk",
        axis=1,
        tiled=True,
    )
    grad_all = grad_all.reshape(
        grad_all.shape[0] * grad_all.shape[1] * grad_all.shape[2], col_width
    )
    one_query = (query_ids[:, None] == jnp.arange(QUERIES, dtype=jnp.int32)[None, :]).astype(
        jnp.bfloat16
    )
    weighted = one_query.T[:, :, None] * query_all[None, :, :]
    query_gram = jnp.einsum(
        "qti,tj->iqj", weighted, query_grad_rot, preferred_element_type=jnp.float32
    )
    norm_scale = float(D * FF) ** (-0.5)
    precond = (query_gram / (eigenvalues[:, None, :] + damping) * norm_scale).astype(jnp.bfloat16)
    precond = precond.reshape(owned_width, QUERIES * col_width)
    shard_rows = lax.all_gather(rotate_blocks(owned_rows, act_basis), "dp", axis=0, tiled=True)
    row_count = shard_rows.shape[0]
    mixed_rows = jnp.dot(shard_rows, precond, preferred_element_type=jnp.float32).reshape(
        row_count, QUERIES, col_width
    )
    token_score = jnp.sum(mixed_rows * grad_all[:, None, :].astype(jnp.float32), axis=2)
    example_count = EX_DP * devices_dp
    one_example = (
        example_ids[:, None] == jnp.arange(example_count, dtype=jnp.int32)[None, :]
    ).astype(jnp.float32)
    partial_scores = jnp.dot(one_example.T, token_score, precision=lax.Precision.HIGHEST)
    all_scores = lax.psum(partial_scores, ("dp", "blk"))
    return lax.dynamic_slice_in_dim(all_scores, lax.axis_index("dp") * EX_DP, EX_DP, 0)


def solution(mesh):
    placed = (
        P(("dp", "blk"), None),
        P(("dp", "blk"), None),
        P("dp", "blk"),
        P("dp", None),
        P("blk", None),
        P(None, "dp"),
        P("blk", "dp"),
        P(),
        P(),
    )
    ndp = mesh.shape["dp"]

    def run(*arrays):
        block = arrays[4].shape[1]
        square = (
            arrays[5].shape[1] == block * ndp
            and arrays[4].shape[0] == 4 * block * mesh.shape["blk"]
            and ndp % PLANE == 0
        )
        return jax.shard_map(
            shards_square if square else shards,
            mesh=mesh, in_specs=placed, out_specs=P("dp", None), check_vma=False
        )(*arrays)

    return run
```

```python
import functools

import jax
import jax.numpy as jnp
from jax import lax
from jax.experimental import pallas as pl
from jax.experimental.pallas import tpu as pltpu
from jax.sharding import PartitionSpec as P

D = 4096
FF = 8192
QUERIES = 16
EX_DP = 2
PLANE = 4
HALVES = 2
MESH = pl.DeviceIdType.MESH


def arrived(ref, sem):
    pltpu.make_async_copy(ref, ref, sem).wait()


def kernel(
    groups, nblk,
    ta, tg, qa, qg, act_basis, grad_basis, eig, qids, eids, out,
    eig_v, ab_v, gb_v, ta_o, qa_o, tg_a, qg_a, tg_o, qg_o, part, parts_a, part_b, parts_b,
    tf, gf, qf, qgf, act, grad, query_t, qmask, weight, even, odd, score, by_query,
    partial, slots_a, red, slots_b,
    load_s, a_s, a_r, p_s, p_r, r_s, r_r,
):
    bf, f32 = jnp.bfloat16, jnp.float32
    dp, blk = lax.axis_index("dp"), lax.axis_index("blk")
    g, p = dp // PLANE, lax.rem(dp, PLANE)
    gb = g * nblk + blk
    column = groups * nblk
    tok, qtok = ta.shape[0], qa.shape[0]
    wa, wh, wg = qa.shape[1], ta_o.shape[-1], tg_o.shape[-1]
    block = ab_v.shape[1]
    across = lax.rem(p + 2, PLANE)
    beside = p + 1 - 2 * lax.rem(p, 2)

    loads = [pltpu.make_async_copy(src, dst, load_s.at[i]) for i, (src, dst) in enumerate(
        ((eig, eig_v), (grad_basis, gb_v), (act_basis, ab_v)))]
    for load in loads:
        load.start()

    in_column = []
    for k in range(1, column):
        to = lax.rem(gb + k, column)
        in_column.append((to // nblk, lax.rem(to, nblk)))
    in_row = [lax.rem(g + k, groups) for k in range(1, groups)]
    in_plane = [lax.rem(p + k, PLANE) for k in range(1, PLANE)]

    barrier = pltpu.get_barrier_semaphore()
    for tg_, tb in in_column:
        pl.semaphore_signal(barrier, inc=1, device_id=(tg_ * PLANE + p, tb), device_id_type=MESH)
    for tp in in_plane:
        pl.semaphore_signal(barrier, inc=1, device_id=(g * PLANE + tp, blk), device_id_type=MESH)
    pl.semaphore_wait(barrier, column - 1 + PLANE - 1)

    def remote(src, dst, send, recv, d, b):
        return pltpu.make_async_remote_copy(
            src, dst, send, recv, device_id=(d, b), device_id_type=MESH)

    def columns(at, width):
        return pl.ds(pl.multiple_of(at, 128), width)

    def send_act(h):
        for tg_ in in_row:
            remote(qa.at[:, h * wh:(h + 1) * wh], qa_o.at[h, p, g], a_s.at[h], a_r.at[h],
                   tg_ * PLANE + p, blk).start()
        pltpu.make_async_copy(
            qa.at[:, h * wh:(h + 1) * wh], qa_o.at[h, p, g], a_r.at[h]).start()
        for tg_, tb in in_column:
            remote(ta.at[:, columns(tb * wa + h * wh, wh)], ta_o.at[h, p, gb],
                   a_s.at[2 + h], a_r.at[2 + h], tg_ * PLANE + p, tb).start()
        pltpu.make_async_copy(
            ta.at[:, columns(blk * wa + h * wh, wh)], ta_o.at[h, p, gb], a_r.at[2 + h]).start()

    send_act(0)
    wide = PLANE * wg
    for tg_ in in_row:
        remote(qg.at[:, columns(tg_ * wide, wide)], qg_a.at[g], a_s.at[4], a_r.at[4],
               tg_ * PLANE + p, blk).start()
    pltpu.make_async_copy(qg.at[:, columns(g * wide, wide)], qg_a.at[g], a_r.at[4]).start()
    for tg_, tb in in_column:
        remote(tg.at[:, columns(tg_ * wide, wide)], tg_a.at[gb], a_s.at[5], a_r.at[5],
               tg_ * PLANE + p, tb).start()
    pltpu.make_async_copy(tg.at[:, columns(g * wide, wide)], tg_a.at[gb], a_r.at[5]).start()

    loads[0].wait()

    def add(i, total):
        rows = eig_v[pl.ds(pl.multiple_of(i * 128, 128), 128), :]
        return total + jnp.sum(rows.reshape(16, 8, rows.shape[1]), axis=0)

    total = lax.fori_loop(
        0, eig_v.shape[0] // 128, add, jnp.zeros((8, eig_v.shape[1]), f32))
    lanes = total[:, 0:128]
    for c in range(1, eig_v.shape[1] // 128):
        lanes = lanes + total[:, c * 128:(c + 1) * 128]
    part[...] = lanes
    for tg_, tb in in_column:
        remote(part, parts_a.at[gb], a_s.at[6], a_r.at[6], tg_ * PLANE + p, tb).start()
    pltpu.make_async_copy(part, parts_a.at[gb], a_r.at[6]).start()

    plane_sends = []

    def to_plane(src, dst, at, tp):
        copy = remote(src, dst, p_s.at[len(plane_sends)], p_r.at[at], g * PLANE + tp, blk)
        plane_sends.append(copy)
        return copy

    early, late = [], []
    for h in range(HALVES):
        early.append([
            to_plane(buf.at[h, p], buf.at[h, p], 12 * h + 2 * i + k, tp)
            for i, buf in enumerate((qa_o, ta_o)) for k, tp in enumerate((across, beside))])
        late.append([
            to_plane(buf.at[h, across], buf.at[h, across], 12 * h + 4 + i, beside)
            for i, buf in enumerate((qa_o, ta_o))])

    def pass_on(h):
        arrived(qa_o.at[h, p], a_r.at[h])
        early[h][0].start()
        early[h][1].start()
        arrived(ta_o.at[h, p], a_r.at[2 + h])
        early[h][2].start()
        early[h][3].start()

    def pass_beside(h):
        arrived(qa_o.at[h, p], p_r.at[12 * h])
        late[h][0].start()
        arrived(ta_o.at[h, p], p_r.at[12 * h + 2])
        late[h][1].start()

    def take(h):
        arrived(qa_o.at[h, p], p_r.at[12 * h + 1])
        arrived(qa_o.at[h, p], p_r.at[12 * h + 4])
        arrived(ta_o.at[h, p], p_r.at[12 * h + 3])
        arrived(ta_o.at[h, p], p_r.at[12 * h + 5])

    def unpack(h):
        for q in range(PLANE):
            for e in range(groups):
                row = (e * PLANE + q) * qtok
                qf[row:row + qtok, :] = qa_o[h, q, e].astype(f32)
                for b in range(nblk):
                    row = ((e * PLANE + q) * nblk + b) * tok
                    tf[row:row + tok, :] = ta_o[h, q, e * nblk + b].astype(f32)

    pass_on(0)
    arrived(qg_a, a_r.at[4])
    for tp in in_plane:
        to_plane(qg_a.at[:, :, columns(tp * wg, wg)], qg_o.at[p], 6, tp).start()
    pltpu.make_async_copy(qg_a.at[:, :, columns(p * wg, wg)], qg_o.at[p], p_r.at[6]).start()
    arrived(tg_a, a_r.at[5])
    for tp in in_plane:
        to_plane(tg_a.at[:, :, columns(tp * wg, wg)], tg_o.at[p], 7, tp).start()
    pltpu.make_async_copy(tg_a.at[:, :, columns(p * wg, wg)], tg_o.at[p], p_r.at[7]).start()
    send_act(1)
    arrived(parts_a, a_r.at[6])
    part_b[...] = jnp.sum(parts_a[...], axis=0)
    for tp in in_plane:
        to_plane(part_b, parts_b.at[p], 8, tp).start()
    pltpu.make_async_copy(part_b, parts_b.at[p], p_r.at[8]).start()
    pass_beside(0)

    loads[1].wait()
    arrived(qg_o, p_r.at[6])
    arrived(tg_o, p_r.at[7])
    for q in range(PLANE):
        for e in range(groups):
            row = (e * PLANE + q) * qtok
            qgf[row:row + qtok, :] = qg_o[q, e].astype(f32)
            for b in range(nblk):
                row = ((e * PLANE + q) * nblk + b) * tok
                gf[row:row + tok, :] = tg_o[q, e * nblk + b].astype(f32)
    turned = jnp.dot(gf[...].astype(bf), gb_v[...], preferred_element_type=f32)
    grad[...] = turned.astype(bf).astype(f32)
    qgrad = jnp.dot(
        qgf[...].astype(bf), gb_v[...], preferred_element_type=f32).astype(bf).astype(f32)
    qtokens = qids.shape[1]
    one_query = (lax.broadcasted_iota(jnp.int32, (QUERIES, qtokens), 0) == qids[...]).astype(f32)
    same = (lax.broadcasted_iota(jnp.int32, (qtokens, qtokens), 0)
            == lax.broadcasted_iota(jnp.int32, (qtokens, qtokens), 1)).astype(f32)
    of_token = lax.dot_general(
        same.astype(bf), one_query.astype(bf), (((1,), (1,)), ((), ())),
        preferred_element_type=f32)
    for q in range(QUERIES):
        qmask[q] = (qgrad * of_token[:, q:q + 1]).astype(bf)
    score[...] = jnp.zeros_like(score)
    loads[2].wait()
    arrived(parts_b, p_r.at[8])
    damping = 0.1 * jnp.sum(parts_b[...]) / (D * FF)
    norm_scale = float(D * FF) ** (-0.5)
    chunk = 256

    count_blocks = wa // block
    in_half = wh // block

    def prepare(n):
        slot = lax.rem(n, 2)
        at = pl.ds(pl.multiple_of(n * block, block), block)
        here = pl.ds(pl.multiple_of(lax.rem(n, in_half) * block, block), block)
        basis = ab_v[at, :]
        turned = jnp.dot(tf[:, here].astype(bf), basis, preferred_element_type=f32)
        act[slot] = turned.astype(bf)
        turned = jnp.dot(qf[:, here].astype(bf), basis, preferred_element_type=f32)
        query_t[slot] = turned.astype(bf).astype(f32).T.astype(bf)
        weight[slot] = norm_scale / (eig_v[at, :] + damping)

    def precondition(at, q, held, cols):
        for r in range(0, block, chunk):
            rows = slice(r, r + chunk)
            gram = jnp.dot(query_t[at, rows, :], qmask[q, :, cols], preferred_element_type=f32)
            held[rows, cols] = (gram * weight[at, rows, cols]).astype(bf)

    def step(at, q, now, later, next_at, next_q, last):
        total = score[q]
        for c in range(0, wg, chunk):
            cols = slice(c, c + chunk)
            mixed = jnp.dot(act[at], now[:, cols], preferred_element_type=f32) * grad[:, cols]
            for k in range(0, chunk, 128):
                total = total + mixed[:, k:k + 128]
            if later is not None:
                precondition(next_at, next_q, later, cols)
        if last:
            lane = lax.broadcasted_iota(jnp.int32, total.shape, 1)
            by_query[...] = jnp.where(
                lane == q, jnp.sum(total, axis=1, keepdims=True), by_query[...])
        else:
            score[q] = total

    def run(at, first, last, final):
        @pl.loop(first, last, step=4)
        def _(q):
            step(at, q, even, odd, at, q + 1, final)
            step(at, q + 1, odd, even, at, q + 2, final)
            step(at, q + 2, even, odd, at, q + 3, final)
            step(at, q + 3, odd, even, at, q + 4, final)

    def tail(at, final):
        q = QUERIES - 4
        step(at, q, even, odd, at, q + 1, final)
        step(at, q + 1, odd, even, at, q + 2, final)
        step(at, q + 2, even, odd, at, q + 3, final)
        step(at, q + 3, odd, None if final else even, 1 - at, 0, final)

    take(0)
    unpack(0)
    by_query[...] = jnp.zeros_like(by_query)
    prepare(0)
    for c in range(0, wg, chunk):
        precondition(0, 0, even, slice(c, c + chunk))

    @pl.loop(0, count_blocks - 1)
    def _(n):
        at = lax.rem(n, 2)
        run(at, 0, QUERIES - 8, False)

        @pl.when(n == 0)
        def _():
            pass_on(1)

        @pl.when(n == 1)
        def _():
            pass_beside(1)

        run(at, QUERIES - 8, QUERIES - 4, False)

        @pl.when(n == in_half - 1)
        def _():
            take(1)
            unpack(1)

        prepare(n + 1)
        tail(at, False)

    run((count_blocks - 1) % 2, 0, QUERIES - 4, True)
    tail((count_blocks - 1) % 2, True)

    examples, tokens = partial.shape[0] * EX_DP, eids.shape[1]
    one = (lax.broadcasted_iota(jnp.int32, (examples, tokens), 0) == eids[...]).astype(f32)
    result = lax.dot_general(
        one, by_query[...], (((1,), (0,)), ((), ())),
        precision=lax.Precision.HIGHEST, preferred_element_type=f32)
    for d in range(partial.shape[0]):
        partial[d] = result[d * EX_DP:(d + 1) * EX_DP, 0:QUERIES]
    for tg_, tb in in_column:
        remote(partial.at[pl.ds(tg_ * PLANE, PLANE)], slots_a.at[gb], r_s.at[0], r_r.at[0],
               tg_ * PLANE + p, tb).start()
    pltpu.make_async_copy(
        partial.at[pl.ds(g * PLANE, PLANE)], slots_a.at[gb], r_r.at[0]).start()
    for copy in plane_sends:
        copy.wait_send()
    for h in range(HALVES):
        arrived(qa_o.at[h, p, 0:groups - 1], a_s.at[h])
        arrived(ta_o.at[h, p, 0:column - 1], a_s.at[2 + h])
    arrived(qg_a.at[0:groups - 1], a_s.at[4])
    arrived(tg_a.at[0:column - 1], a_s.at[5])
    arrived(parts_a.at[0:column - 1], a_s.at[6])
    arrived(slots_a, r_r.at[0])
    red[...] = jnp.sum(slots_a[...], axis=0)
    for tp in in_plane:
        remote(red.at[tp], slots_b.at[p], r_s.at[1], r_r.at[1], g * PLANE + tp, blk).start()
    pltpu.make_async_copy(red.at[p], slots_b.at[p], r_r.at[1]).start()
    arrived(slots_a.at[0:column - 1], r_s.at[0])
    arrived(slots_b, r_r.at[1])
    arrived(slots_b.at[0:PLANE - 1], r_s.at[1])
    out[...] = jnp.sum(slots_b[...], axis=0)


def shards_square(
    ta, tg, qa, qg, act_basis, grad_basis, eig, example_ids, query_ids,
):
    ndp, nblk = lax.axis_size("dp"), lax.axis_size("blk")
    groups = ndp // PLANE
    column = groups * nblk
    tok, qtok = ta.shape[0], qa.shape[0]
    wa, wg = qa.shape[1], tg.shape[1] // ndp
    wh = wa // HALVES
    block = act_basis.shape[1]
    tokens, qtokens = ndp * nblk * tok, ndp * qtok
    bf, f32 = jnp.bfloat16, jnp.float32
    dma = pltpu.SemaphoreType.DMA
    vmem = pltpu.VMEM
    full = pl.BlockSpec(memory_space=pltpu.VMEM)
    far = pl.BlockSpec(memory_space=pl.ANY)
    return pl.pallas_call(
        functools.partial(kernel, groups, nblk),
        out_shape=jax.ShapeDtypeStruct((EX_DP, QUERIES), f32),
        in_specs=[far] * 7 + [full] * 2,
        out_specs=full,
        scratch_shapes=[
            vmem(eig.shape, f32), vmem(act_basis.shape, bf), vmem(grad_basis.shape, bf),
            vmem((HALVES, PLANE, column, tok, wh), bf),
            vmem((HALVES, PLANE, groups, qtok, wh), bf),
            vmem((column, tok, PLANE * wg), bf), vmem((groups, qtok, PLANE * wg), bf),
            vmem((PLANE, column, tok, wg), bf), vmem((PLANE, groups, qtok, wg), bf),
            vmem((8, 128), f32), vmem((column, 8, 128), f32),
            vmem((8, 128), f32), vmem((PLANE, 8, 128), f32),
            vmem((tokens, wh), f32), vmem((tokens, wg), f32),
            vmem((qtokens, wh), f32), vmem((qtokens, wg), f32),
            vmem((2, tokens, block), bf), vmem((tokens, wg), f32),
            vmem((2, block, qtokens), bf), vmem((QUERIES, qtokens, wg), bf),
            vmem((2, block, wg), f32), vmem((block, wg), bf), vmem((block, wg), bf),
            vmem((QUERIES, tokens, 128), f32), vmem((tokens, 128), f32),
            vmem((ndp, EX_DP, QUERIES), f32), vmem((column, PLANE, EX_DP, QUERIES), f32),
            vmem((PLANE, EX_DP, QUERIES), f32), vmem((PLANE, EX_DP, QUERIES), f32),
            dma((3,)), dma((7,)), dma((7,)), dma((32,)), dma((20,)),
            dma((2,)), dma((2,)),
        ],
        compiler_params=pltpu.CompilerParams(
            collective_id=0, has_side_effects=True, vmem_limit_bytes=56 * 2**20
        ),
        name="influence",
    )(ta, tg, qa, qg, act_basis, grad_basis, eig, query_ids[None, :], example_ids[None, :])


def as_sent(x):

    def short(part):
        return part.astype(jnp.bfloat16) if part.dtype == jnp.float32 else part

    return jax.tree.map(short, x)


def partner(block, axis, stride):
    count = lax.axis_size(axis)
    route = []
    for low in range(count):
        high = low | 1 << stride
        if high != low and high < count:
            route += [(low, high), (high, low)]
    return lax.ppermute(block, axis, route)


def rotate_blocks(row_data, basis):
    row_count = row_data.shape[0]
    block_size = basis.shape[1]
    count_blocks = basis.shape[0] // block_size
    turned = jnp.einsum(
        "tnk,nkl->tnl",
        row_data.reshape(row_count, count_blocks, block_size),
        basis.reshape(count_blocks, block_size, block_size),
        preferred_element_type=jnp.float32,
    )
    return turned.reshape(row_count, count_blocks * block_size).astype(jnp.bfloat16)


def rotate_columns(row_data, basis):
    row_count = row_data.shape[0]
    full_width = row_data.shape[1]
    block_size = basis.shape[0]
    col_width = basis.shape[1]
    count_blocks = full_width // block_size
    turned = jnp.einsum(
        "tmk,kml->tml",
        row_data.reshape(row_count, count_blocks, block_size),
        basis.reshape(block_size, count_blocks, col_width // count_blocks),
        preferred_element_type=jnp.float32,
    )
    return turned.reshape(row_count, col_width).astype(jnp.bfloat16)


def join_pair(mine, other, is_upper):
    return jnp.where(is_upper, jnp.concatenate([other, mine], 1), jnp.concatenate([mine, other], 1))


def shards(
    train_act,
    train_grad,
    query_act,
    query_grad,
    act_basis,
    grad_basis,
    eigenvalues,
    example_ids,
    query_ids,
):
    devices_dp = lax.axis_size("dp")
    block_size = grad_basis.shape[0]
    col_width = grad_basis.shape[1]
    owned_width = act_basis.shape[0]
    eigen_sum = lax.psum(jnp.sum(eigenvalues), ("dp", "blk"))
    damping = 0.1 * eigen_sum / (D * FF)
    owned_rows = lax.all_to_all(train_act, "blk", split_axis=1, concat_axis=0, tiled=True)
    query_all = lax.all_gather(rotate_blocks(query_act, act_basis), "dp", axis=0, tiled=True)
    train_cols, query_cols = (
        lax.all_to_all(train_grad, "dp", split_axis=1, concat_axis=0, tiled=True),
        lax.all_to_all(query_grad, "dp", split_axis=1, concat_axis=0, tiled=True),
    )
    if col_width < block_size:
        position = lax.axis_index("dp")
        for bit_index in range((block_size // col_width).bit_length() - 1):
            other_train, other_query = (
                partner(as_sent(train_cols), "dp", bit_index).astype(train_cols.dtype),
                partner(as_sent(query_cols), "dp", bit_index).astype(query_cols.dtype),
            )
            is_upper = position >> bit_index & 1 == 1
            train_cols = join_pair(train_cols, other_train, is_upper)
            query_cols = join_pair(query_cols, other_query, is_upper)
    grad_mine = rotate_columns(train_cols, grad_basis)
    query_grad_rot = rotate_columns(query_cols, grad_basis)
    grad_all = lax.all_gather(
        grad_mine.reshape(devices_dp, 1, grad_mine.shape[0] // devices_dp, col_width),
        "blk",
        axis=1,
        tiled=True,
    )
    grad_all = grad_all.reshape(
        grad_all.shape[0] * grad_all.shape[1] * grad_all.shape[2], col_width
    )
    one_query = (query_ids[:, None] == jnp.arange(QUERIES, dtype=jnp.int32)[None, :]).astype(
        jnp.bfloat16
    )
    weighted = one_query.T[:, :, None] * query_all[None, :, :]
    query_gram = jnp.einsum(
        "qti,tj->iqj", weighted, query_grad_rot, preferred_element_type=jnp.float32
    )
    norm_scale = float(D * FF) ** (-0.5)
    precond = (query_gram / (eigenvalues[:, None, :] + damping) * norm_scale).astype(jnp.bfloat16)
    precond = precond.reshape(owned_width, QUERIES * col_width)
    shard_rows = lax.all_gather(rotate_blocks(owned_rows, act_basis), "dp", axis=0, tiled=True)
    row_count = shard_rows.shape[0]
    mixed_rows = jnp.dot(shard_rows, precond, preferred_element_type=jnp.float32).reshape(
        row_count, QUERIES, col_width
    )
    token_score = jnp.sum(mixed_rows * grad_all[:, None, :].astype(jnp.float32), axis=2)
    example_count = EX_DP * devices_dp
    one_example = (
        example_ids[:, None] == jnp.arange(example_count, dtype=jnp.int32)[None, :]
    ).astype(jnp.float32)
    partial_scores = jnp.dot(one_example.T, token_score, precision=lax.Precision.HIGHEST)
    all_scores = lax.psum(partial_scores, ("dp", "blk"))
    return lax.dynamic_slice_in_dim(all_scores, lax.axis_index("dp") * EX_DP, EX_DP, 0)


def solution(mesh):
    placed = (
        P(("dp", "blk"), None),
        P(("dp", "blk"), None),
        P("dp", "blk"),
        P("dp", None),
        P("blk", None),
        P(None, "dp"),
        P("blk", "dp"),
        P(),
        P(),
    )
    ndp = mesh.shape["dp"]

    def run(*arrays):
        block = arrays[4].shape[1]
        square = (
            arrays[5].shape[1] == block * ndp
            and arrays[4].shape[0] == 4 * block * mesh.shape["blk"]
            and ndp % PLANE == 0
        )
        return jax.shard_map(
            shards_square if square else shards,
            mesh=mesh, in_specs=placed, out_specs=P("dp", None), check_vma=False
        )(*arrays)

    return run
```

```python
import functools

import jax
import jax.numpy as jnp
from jax import lax
from jax.experimental import pallas as pl
from jax.experimental.pallas import tpu as pltpu
from jax.sharding import PartitionSpec as P

D = 4096
FF = 8192
QUERIES = 16
EX_DP = 2
PLANE = 4
HALVES = 2
MESH = pl.DeviceIdType.MESH


def arrived(ref, sem):
    pltpu.make_async_copy(ref, ref, sem).wait()


def kernel(
    groups, nblk,
    ta, tg, qa, qg, act_basis, grad_basis, eig, qids, eids, out,
    eig_v, ab_v, gb_v, ta_o, qa_o, tg_a, qg_a, tg_o, qg_o, part, parts_a, part_b, parts_b,
    tf, gf, qf, qgf, act, grad, query_t, qmask, weight, even, odd, score, by_query,
    partial, slots_a, red, slots_b,
    load_s, a_s, a_r, p_s, p_r, r_s, r_r,
):
    bf, f32 = jnp.bfloat16, jnp.float32
    dp, blk = lax.axis_index("dp"), lax.axis_index("blk")
    g, p = dp // PLANE, lax.rem(dp, PLANE)
    gb = g * nblk + blk
    column = groups * nblk
    tok, qtok = ta.shape[0], qa.shape[0]
    wa, wh, wg = qa.shape[1], ta_o.shape[-1], tg_o.shape[-1]
    block = ab_v.shape[1]
    across = lax.rem(p + 2, PLANE)
    beside = p + 1 - 2 * lax.rem(p, 2)

    loads = [pltpu.make_async_copy(src, dst, load_s.at[i]) for i, (src, dst) in enumerate(
        ((eig, eig_v), (grad_basis, gb_v), (act_basis, ab_v)))]
    for load in loads:
        load.start()

    in_column = []
    for k in range(1, column):
        to = lax.rem(gb + k, column)
        in_column.append((to // nblk, lax.rem(to, nblk)))
    in_row = [lax.rem(g + k, groups) for k in range(1, groups)]
    in_plane = [lax.rem(p + k, PLANE) for k in range(1, PLANE)]

    other_blk = [lax.rem(blk + k, nblk) for k in range(1, nblk)]

    barrier = pltpu.get_barrier_semaphore()
    for tg_, tb in in_column:
        pl.semaphore_signal(barrier, inc=1, device_id=(tg_ * PLANE + p, tb), device_id_type=MESH)
    for tp in in_plane:
        pl.semaphore_signal(barrier, inc=1, device_id=(g * PLANE + tp, blk), device_id_type=MESH)
        for tb in other_blk:
            pl.semaphore_signal(
                barrier, inc=1, device_id=(g * PLANE + tp, tb), device_id_type=MESH)
    pl.semaphore_wait(barrier, column - 1 + (PLANE - 1) * nblk)

    def remote(src, dst, send, recv, d, b):
        return pltpu.make_async_remote_copy(
            src, dst, send, recv, device_id=(d, b), device_id_type=MESH)

    def columns(at, width):
        return pl.ds(pl.multiple_of(at, 128), width)

    def send_act(h):
        for tg_ in in_row:
            remote(qa.at[:, h * wh:(h + 1) * wh], qa_o.at[h, p, g], a_s.at[h], a_r.at[h],
                   tg_ * PLANE + p, blk).start()
        pltpu.make_async_copy(
            qa.at[:, h * wh:(h + 1) * wh], qa_o.at[h, p, g], a_r.at[h]).start()
        for tg_, tb in in_column:
            remote(ta.at[:, columns(tb * wa + h * wh, wh)], ta_o.at[h, p, gb],
                   a_s.at[2 + h], a_r.at[2 + h], tg_ * PLANE + p, tb).start()
        pltpu.make_async_copy(
            ta.at[:, columns(blk * wa + h * wh, wh)], ta_o.at[h, p, gb], a_r.at[2 + h]).start()

    send_act(0)
    wide = PLANE * wg
    for tg_ in in_row:
        remote(qg.at[:, columns(tg_ * wide, wide)], qg_a.at[g], a_s.at[4], a_r.at[4],
               tg_ * PLANE + p, blk).start()
    pltpu.make_async_copy(qg.at[:, columns(g * wide, wide)], qg_a.at[g], a_r.at[4]).start()
    for tg_ in in_row:
        remote(tg.at[:, columns(tg_ * wide, wide)], tg_a.at[g], a_s.at[5], a_r.at[5],
               tg_ * PLANE + p, blk).start()
    pltpu.make_async_copy(tg.at[:, columns(g * wide, wide)], tg_a.at[g], a_r.at[5]).start()

    loads[0].wait()

    def add(i, total):
        rows = eig_v[pl.ds(pl.multiple_of(i * 128, 128), 128), :]
        return total + jnp.sum(rows.reshape(16, 8, rows.shape[1]), axis=0)

    total = lax.fori_loop(
        0, eig_v.shape[0] // 128, add, jnp.zeros((8, eig_v.shape[1]), f32))
    lanes = total[:, 0:128]
    for c in range(1, eig_v.shape[1] // 128):
        lanes = lanes + total[:, c * 128:(c + 1) * 128]
    part[...] = lanes
    for tg_, tb in in_column:
        remote(part, parts_a.at[gb], a_s.at[6], a_r.at[6], tg_ * PLANE + p, tb).start()
    pltpu.make_async_copy(part, parts_a.at[gb], a_r.at[6]).start()

    plane_sends = []

    def to_plane(src, dst, at, tp, b=blk):
        copy = remote(src, dst, p_s.at[len(plane_sends)], p_r.at[at], g * PLANE + tp, b)
        plane_sends.append(copy)
        return copy

    early, late = [], []
    for h in range(HALVES):
        early.append([
            to_plane(buf.at[h, p], buf.at[h, p], 12 * h + 2 * i + k, tp)
            for i, buf in enumerate((qa_o, ta_o)) for k, tp in enumerate((across, beside))])
        late.append([
            to_plane(buf.at[h, across], buf.at[h, across], 12 * h + 4 + i, beside)
            for i, buf in enumerate((qa_o, ta_o))])

    def pass_on(h):
        arrived(qa_o.at[h, p], a_r.at[h])
        early[h][0].start()
        early[h][1].start()
        arrived(ta_o.at[h, p], a_r.at[2 + h])
        early[h][2].start()
        early[h][3].start()

    def pass_beside(h):
        arrived(qa_o.at[h, p], p_r.at[12 * h])
        late[h][0].start()
        arrived(ta_o.at[h, p], p_r.at[12 * h + 2])
        late[h][1].start()

    def take(h):
        arrived(qa_o.at[h, p], p_r.at[12 * h + 1])
        arrived(qa_o.at[h, p], p_r.at[12 * h + 4])
        arrived(ta_o.at[h, p], p_r.at[12 * h + 3])
        arrived(ta_o.at[h, p], p_r.at[12 * h + 5])

    def unpack(h):
        for q in range(PLANE):
            for e in range(groups):
                row = (e * PLANE + q) * qtok
                qf[row:row + qtok, :] = qa_o[h, q, e].astype(f32)
                for b in range(nblk):
                    row = ((e * PLANE + q) * nblk + b) * tok
                    tf[row:row + tok, :] = ta_o[h, q, e * nblk + b].astype(f32)

    pass_on(0)
    arrived(qg_a, a_r.at[4])
    for tp in in_plane:
        to_plane(qg_a.at[:, :, columns(tp * wg, wg)], qg_o.at[p], 6, tp).start()
    pltpu.make_async_copy(qg_a.at[:, :, columns(p * wg, wg)], qg_o.at[p], p_r.at[6]).start()
    arrived(tg_a, a_r.at[5])
    for tp in in_plane:
        to_plane(tg_a.at[:, :, columns(tp * wg, wg)], tg_o.at[p, blk], 7, tp).start()
    for tb in other_blk:
        for tp in [p] + in_plane:
            to_plane(tg_a.at[:, :, columns(tp * wg, wg)], tg_o.at[p, blk], 7, tp, tb).start()
    pltpu.make_async_copy(
        tg_a.at[:, :, columns(p * wg, wg)], tg_o.at[p, blk], p_r.at[7]).start()
    send_act(1)
    arrived(parts_a, a_r.at[6])
    part_b[...] = jnp.sum(parts_a[...], axis=0)
    for tp in in_plane:
        to_plane(part_b, parts_b.at[p], 8, tp).start()
    pltpu.make_async_copy(part_b, parts_b.at[p], p_r.at[8]).start()
    pass_beside(0)

    loads[1].wait()
    arrived(qg_o, p_r.at[6])
    arrived(tg_o, p_r.at[7])
    for q in range(PLANE):
        for e in range(groups):
            row = (e * PLANE + q) * qtok
            qgf[row:row + qtok, :] = qg_o[q, e].astype(f32)
            for b in range(nblk):
                row = ((e * PLANE + q) * nblk + b) * tok
                gf[row:row + tok, :] = tg_o[q, b, e].astype(f32)
    turned = jnp.dot(gf[...].astype(bf), gb_v[...], preferred_element_type=f32)
    grad[...] = turned.astype(bf).astype(f32)
    qgrad = jnp.dot(
        qgf[...].astype(bf), gb_v[...], preferred_element_type=f32).astype(bf).astype(f32)
    qtokens = qids.shape[1]
    one_query = (lax.broadcasted_iota(jnp.int32, (QUERIES, qtokens), 0) == qids[...]).astype(f32)
    same = (lax.broadcasted_iota(jnp.int32, (qtokens, qtokens), 0)
            == lax.broadcasted_iota(jnp.int32, (qtokens, qtokens), 1)).astype(f32)
    of_token = lax.dot_general(
        same.astype(bf), one_query.astype(bf), (((1,), (1,)), ((), ())),
        preferred_element_type=f32)
    for q in range(QUERIES):
        qmask[q] = (qgrad * of_token[:, q:q + 1]).astype(bf)
    score[...] = jnp.zeros_like(score)
    loads[2].wait()
    arrived(parts_b, p_r.at[8])
    damping = 0.1 * jnp.sum(parts_b[...]) / (D * FF)
    norm_scale = float(D * FF) ** (-0.5)
    chunk = 256

    count_blocks = wa // block
    in_half = wh // block

    def prepare(n):
        slot = lax.rem(n, 2)
        at = pl.ds(pl.multiple_of(n * block, block), block)
        here = pl.ds(pl.multiple_of(lax.rem(n, in_half) * block, block), block)
        basis = ab_v[at, :]
        turned = jnp.dot(tf[:, here].astype(bf), basis, preferred_element_type=f32)
        act[slot] = turned.astype(bf)
        turned = jnp.dot(qf[:, here].astype(bf), basis, preferred_element_type=f32)
        query_t[slot] = turned.astype(bf).astype(f32).T.astype(bf)
        weight[slot] = norm_scale / (eig_v[at, :] + damping)

    def precondition(at, q, held, rows):
        for c in range(0, wg, chunk):
            cols = slice(c, c + chunk)
            gram = jnp.dot(query_t[at, rows, :], qmask[q, :, cols], preferred_element_type=f32)
            held[rows, cols] = (gram * weight[at, rows, cols]).astype(bf)

    def step(at, q, now, later, next_at, next_q, last):
        mixed = None
        for c in range(0, block, chunk):
            rows = slice(c, c + chunk)
            term = jnp.dot(act[at, :, rows], now[rows, :], preferred_element_type=f32)
            if later is not None:
                precondition(next_at, next_q, later, rows)
            mixed = term if mixed is None else mixed + term
        mixed = mixed * grad[...]
        total = score[q]
        for c in range(0, wg, 128):
            total = total + mixed[:, c:c + 128]
        if last:
            lane = lax.broadcasted_iota(jnp.int32, total.shape, 1)
            by_query[...] = jnp.where(
                lane == q, jnp.sum(total, axis=1, keepdims=True), by_query[...])
        else:
            score[q] = total

    def run(at, first, last, final):
        @pl.loop(first, last, step=4)
        def _(q):
            step(at, q, even, odd, at, q + 1, final)
            step(at, q + 1, odd, even, at, q + 2, final)
            step(at, q + 2, even, odd, at, q + 3, final)
            step(at, q + 3, odd, even, at, q + 4, final)

    def tail(at, final):
        q = QUERIES - 4
        step(at, q, even, odd, at, q + 1, final)
        step(at, q + 1, odd, even, at, q + 2, final)
        step(at, q + 2, even, odd, at, q + 3, final)
        step(at, q + 3, odd, None if final else even, 1 - at, 0, final)

    take(0)
    unpack(0)
    by_query[...] = jnp.zeros_like(by_query)
    prepare(0)
    for c in range(0, block, chunk):
        precondition(0, 0, even, slice(c, c + chunk))

    @pl.loop(0, count_blocks - 1)
    def _(n):
        at = lax.rem(n, 2)
        run(at, 0, QUERIES - 8, False)

        @pl.when(n == 0)
        def _():
            pass_on(1)

        @pl.when(n == 1)
        def _():
            pass_beside(1)

        run(at, QUERIES - 8, QUERIES - 4, False)

        @pl.when(n == in_half - 1)
        def _():
            take(1)
            unpack(1)

        prepare(n + 1)
        tail(at, False)

    run((count_blocks - 1) % 2, 0, QUERIES - 4, True)
    tail((count_blocks - 1) % 2, True)

    examples, tokens = partial.shape[0] * EX_DP, eids.shape[1]
    one = (lax.broadcasted_iota(jnp.int32, (examples, tokens), 0) == eids[...]).astype(f32)
    result = lax.dot_general(
        one, by_query[...], (((1,), (0,)), ((), ())),
        precision=lax.Precision.HIGHEST, preferred_element_type=f32)
    for d in range(partial.shape[0]):
        partial[d] = result[d * EX_DP:(d + 1) * EX_DP, 0:QUERIES]
    for tg_, tb in in_column:
        remote(partial.at[pl.ds(tg_ * PLANE, PLANE)], slots_a.at[gb], r_s.at[0], r_r.at[0],
               tg_ * PLANE + p, tb).start()
    pltpu.make_async_copy(
        partial.at[pl.ds(g * PLANE, PLANE)], slots_a.at[gb], r_r.at[0]).start()
    for copy in plane_sends:
        copy.wait_send()
    for h in range(HALVES):
        arrived(qa_o.at[h, p, 0:groups - 1], a_s.at[h])
        arrived(ta_o.at[h, p, 0:column - 1], a_s.at[2 + h])
    arrived(qg_a.at[0:groups - 1], a_s.at[4])
    arrived(tg_a.at[0:groups - 1], a_s.at[5])
    arrived(parts_a.at[0:column - 1], a_s.at[6])
    arrived(slots_a, r_r.at[0])
    red[...] = jnp.sum(slots_a[...], axis=0)
    for tp in in_plane:
        remote(red.at[tp], slots_b.at[p], r_s.at[1], r_r.at[1], g * PLANE + tp, blk).start()
    pltpu.make_async_copy(red.at[p], slots_b.at[p], r_r.at[1]).start()
    arrived(slots_a.at[0:column - 1], r_s.at[0])
    arrived(slots_b, r_r.at[1])
    arrived(slots_b.at[0:PLANE - 1], r_s.at[1])
    out[...] = jnp.sum(slots_b[...], axis=0)


def shards_square(
    ta, tg, qa, qg, act_basis, grad_basis, eig, example_ids, query_ids,
):
    ndp, nblk = lax.axis_size("dp"), lax.axis_size("blk")
    groups = ndp // PLANE
    column = groups * nblk
    tok, qtok = ta.shape[0], qa.shape[0]
    wa, wg = qa.shape[1], tg.shape[1] // ndp
    wh = wa // HALVES
    block = act_basis.shape[1]
    tokens, qtokens = ndp * nblk * tok, ndp * qtok
    bf, f32 = jnp.bfloat16, jnp.float32
    dma = pltpu.SemaphoreType.DMA
    vmem = pltpu.VMEM
    full = pl.BlockSpec(memory_space=pltpu.VMEM)
    far = pl.BlockSpec(memory_space=pl.ANY)
    return pl.pallas_call(
        functools.partial(kernel, groups, nblk),
        out_shape=jax.ShapeDtypeStruct((EX_DP, QUERIES), f32),
        in_specs=[far] * 7 + [full] * 2,
        out_specs=full,
        scratch_shapes=[
            vmem(eig.shape, f32), vmem(act_basis.shape, bf), vmem(grad_basis.shape, bf),
            vmem((HALVES, PLANE, column, tok, wh), bf),
            vmem((HALVES, PLANE, groups, qtok, wh), bf),
            vmem((groups, tok, PLANE * wg), bf), vmem((groups, qtok, PLANE * wg), bf),
            vmem((PLANE, nblk, groups, tok, wg), bf), vmem((PLANE, groups, qtok, wg), bf),
            vmem((8, 128), f32), vmem((column, 8, 128), f32),
            vmem((8, 128), f32), vmem((PLANE, 8, 128), f32),
            vmem((tokens, wh), f32), vmem((tokens, wg), f32),
            vmem((qtokens, wh), f32), vmem((qtokens, wg), f32),
            vmem((2, tokens, block), bf), vmem((tokens, wg), f32),
            vmem((2, block, qtokens), bf), vmem((QUERIES, qtokens, wg), bf),
            vmem((2, block, wg), f32), vmem((block, wg), bf), vmem((block, wg), bf),
            vmem((QUERIES, tokens, 128), f32), vmem((tokens, 128), f32),
            vmem((ndp, EX_DP, QUERIES), f32), vmem((column, PLANE, EX_DP, QUERIES), f32),
            vmem((PLANE, EX_DP, QUERIES), f32), vmem((PLANE, EX_DP, QUERIES), f32),
            dma((3,)), dma((7,)), dma((7,)), dma((17 + PLANE * (nblk + 1),)), dma((20,)),
            dma((2,)), dma((2,)),
        ],
        compiler_params=pltpu.CompilerParams(
            collective_id=0, has_side_effects=True, vmem_limit_bytes=56 * 2**20
        ),
        name="influence",
    )(ta, tg, qa, qg, act_basis, grad_basis, eig, query_ids[None, :], example_ids[None, :])


def as_sent(x):

    def short(part):
        return part.astype(jnp.bfloat16) if part.dtype == jnp.float32 else part

    return jax.tree.map(short, x)


def partner(block, axis, stride):
    count = lax.axis_size(axis)
    route = []
    for low in range(count):
        high = low | 1 << stride
        if high != low and high < count:
            route += [(low, high), (high, low)]
    return lax.ppermute(block, axis, route)


def rotate_blocks(row_data, basis):
    row_count = row_data.shape[0]
    block_size = basis.shape[1]
    count_blocks = basis.shape[0] // block_size
    turned = jnp.einsum(
        "tnk,nkl->tnl",
        row_data.reshape(row_count, count_blocks, block_size),
        basis.reshape(count_blocks, block_size, block_size),
        preferred_element_type=jnp.float32,
    )
    return turned.reshape(row_count, count_blocks * block_size).astype(jnp.bfloat16)


def rotate_columns(row_data, basis):
    row_count = row_data.shape[0]
    full_width = row_data.shape[1]
    block_size = basis.shape[0]
    col_width = basis.shape[1]
    count_blocks = full_width // block_size
    turned = jnp.einsum(
        "tmk,kml->tml",
        row_data.reshape(row_count, count_blocks, block_size),
        basis.reshape(block_size, count_blocks, col_width // count_blocks),
        preferred_element_type=jnp.float32,
    )
    return turned.reshape(row_count, col_width).astype(jnp.bfloat16)


def join_pair(mine, other, is_upper):
    return jnp.where(is_upper, jnp.concatenate([other, mine], 1), jnp.concatenate([mine, other], 1))


def shards(
    train_act,
    train_grad,
    query_act,
    query_grad,
    act_basis,
    grad_basis,
    eigenvalues,
    example_ids,
    query_ids,
):
    devices_dp = lax.axis_size("dp")
    block_size = grad_basis.shape[0]
    col_width = grad_basis.shape[1]
    owned_width = act_basis.shape[0]
    eigen_sum = lax.psum(jnp.sum(eigenvalues), ("dp", "blk"))
    damping = 0.1 * eigen_sum / (D * FF)
    owned_rows = lax.all_to_all(train_act, "blk", split_axis=1, concat_axis=0, tiled=True)
    query_all = lax.all_gather(rotate_blocks(query_act, act_basis), "dp", axis=0, tiled=True)
    train_cols, query_cols = (
        lax.all_to_all(train_grad, "dp", split_axis=1, concat_axis=0, tiled=True),
        lax.all_to_all(query_grad, "dp", split_axis=1, concat_axis=0, tiled=True),
    )
    if col_width < block_size:
        position = lax.axis_index("dp")
        for bit_index in range((block_size // col_width).bit_length() - 1):
            other_train, other_query = (
                partner(as_sent(train_cols), "dp", bit_index).astype(train_cols.dtype),
                partner(as_sent(query_cols), "dp", bit_index).astype(query_cols.dtype),
            )
            is_upper = position >> bit_index & 1 == 1
            train_cols = join_pair(train_cols, other_train, is_upper)
            query_cols = join_pair(query_cols, other_query, is_upper)
    grad_mine = rotate_columns(train_cols, grad_basis)
    query_grad_rot = rotate_columns(query_cols, grad_basis)
    grad_all = lax.all_gather(
        grad_mine.reshape(devices_dp, 1, grad_mine.shape[0] // devices_dp, col_width),
        "blk",
        axis=1,
        tiled=True,
    )
    grad_all = grad_all.reshape(
        grad_all.shape[0] * grad_all.shape[1] * grad_all.shape[2], col_width
    )
    one_query = (query_ids[:, None] == jnp.arange(QUERIES, dtype=jnp.int32)[None, :]).astype(
        jnp.bfloat16
    )
    weighted = one_query.T[:, :, None] * query_all[None, :, :]
    query_gram = jnp.einsum(
        "qti,tj->iqj", weighted, query_grad_rot, preferred_element_type=jnp.float32
    )
    norm_scale = float(D * FF) ** (-0.5)
    precond = (query_gram / (eigenvalues[:, None, :] + damping) * norm_scale).astype(jnp.bfloat16)
    precond = precond.reshape(owned_width, QUERIES * col_width)
    shard_rows = lax.all_gather(rotate_blocks(owned_rows, act_basis), "dp", axis=0, tiled=True)
    row_count = shard_rows.shape[0]
    mixed_rows = jnp.dot(shard_rows, precond, preferred_element_type=jnp.float32).reshape(
        row_count, QUERIES, col_width
    )
    token_score = jnp.sum(mixed_rows * grad_all[:, None, :].astype(jnp.float32), axis=2)
    example_count = EX_DP * devices_dp
    one_example = (
        example_ids[:, None] == jnp.arange(example_count, dtype=jnp.int32)[None, :]
    ).astype(jnp.float32)
    partial_scores = jnp.dot(one_example.T, token_score, precision=lax.Precision.HIGHEST)
    all_scores = lax.psum(partial_scores, ("dp", "blk"))
    return lax.dynamic_slice_in_dim(all_scores, lax.axis_index("dp") * EX_DP, EX_DP, 0)


def solution(mesh):
    placed = (
        P(("dp", "blk"), None),
        P(("dp", "blk"), None),
        P("dp", "blk"),
        P("dp", None),
        P("blk", None),
        P(None, "dp"),
        P("blk", "dp"),
        P(),
        P(),
    )
    ndp = mesh.shape["dp"]

    def run(*arrays):
        block = arrays[4].shape[1]
        square = (
            arrays[5].shape[1] == block * ndp
            and arrays[4].shape[0] == 4 * block * mesh.shape["blk"]
            and ndp % PLANE == 0
        )
        return jax.shard_map(
            shards_square if square else shards,
            mesh=mesh, in_specs=placed, out_specs=P("dp", None), check_vma=False
        )(*arrays)

    return run
```
